32 devices in a mesh: gx: 16 (over z, y, core), az: 2 (over x).
Axes of the slice: x: 2, y: 2, z: 4, core: 2. Of those that a mesh axis runs over, the one named last changes fastest.
Arguments:
- state: float32 [5, 256, 256, 512], P(None, 'gx', 'az'), as said below
- sponge_level: int32 [256, 256, 512], P('gx', 'az'), may hold values from 0 to 3
- inv_dx: float32 [256], P('gx'), may hold values from 1 to 8
- inv_dr: float32 [512], replicated, may hold values from 1 to 8
- target: float32 [5, 512], replicated, may hold values from -4 to 4
- cutoff: int32 [32], replicated, may hold values from 2 to 32, as said below
Outputs:
- section_state: float32 [5, 256, 256, 512], P(None, 'gx', 'az')
The draws below stay inside these ranges and needn't reach their ends.
Inputs may be any that keep to these rules, and one draw needn't show every extreme that they name: `cutoff`: every value from 2 to 32 may occur; both ends occur on some cycle. `state`: density lies between 0.7 and 1.3 and pressure is positive.
All inputs are finite; a program needn't handle non-finite values.
Results may differ from the reference program's by a relative error of at most 0.0003.
Values sent between devices are 32-bit elements; how exact they have to be, the bound alone decides.
No kernel may reach another device: no remote copies, remote signals or barrier semaphores. Data moves between devices by JAX's collectives and lax.ppermute only.
A program may use at most 320 MiB of HBM per device.

```python
import math
import jax
import jax.numpy as jnp
from jax import lax

NT = 256
NR = 512
CYCLE = 32
PL_DEV = 16
NX = 256


def draw_state(key, part):
    keys = jax.random.split(key, 5)
    shape = (NX, NT, NR)
    noise_a = jnp.clip(jax.random.normal(keys[0], shape, jnp.float32), -4.0, 4.0)
    noise_b = jnp.clip(jax.random.normal(keys[1], shape, jnp.float32), -4.0, 4.0)
    noise_c = jnp.clip(jax.random.normal(keys[2], shape, jnp.float32), -4.0, 4.0)
    density = 0.7 + 0.6 * jax.random.uniform(keys[3], shape, jnp.float32)
    pressure = 0.7 + 0.6 * jax.random.uniform(keys[4], shape, jnp.float32)
    axial_momentum = density * (0.9 + 0.3 * noise_a)
    radial_momentum = 0.3 * noise_b
    swirl_momentum = 0.3 * noise_c
    energy = pressure / 0.4 + 0.5 * (axial_momentum * axial_momentum + radial_momentum * radial_momentum + swirl_momentum * swirl_momentum) / density
    return jnp.stack([density, axial_momentum, radial_momentum, swirl_momentum, energy]).astype(jnp.float32)


def draw_cutoff(key, part):
    keys = jax.random.split(key, 3)
    highest = NT // 8
    values = jax.random.randint(keys[0], (CYCLE,), 2, highest + 1)
    first_cycle = jax.random.randint(keys[1], (), 0, CYCLE)
    second_cycle = (first_cycle + jax.random.randint(keys[2], (), 1, CYCLE)) % CYCLE
    values = values.at[first_cycle].set(highest).at[second_cycle].set(2)
    return values.astype(jnp.int32)


def with_ends(drawn, key, low, top_value):
    index_at = [jax.random.randint(jax.random.fold_in(key, axis), (), 0, length) for axis, length in enumerate(drawn.shape)]
    longest = drawn.shape.index(max(drawn.shape))
    neighbour = index_at[:longest] + [(index_at[longest] + 1) % drawn.shape[longest]] + index_at[longest + 1:]
    return drawn.at[tuple(index_at)].set(low).at[tuple(neighbour)].set(top_value)


def steps_of(key, extent, cuts, low, largest):
    def one(axis_at, parts):
        steps = jax.random.uniform(jax.random.fold_in(jax.random.fold_in(key, 6), axis_at), (parts,), jnp.float32, low / len(cuts), largest / len(cuts))
        return jnp.repeat(jnp.exp(steps), extent[axis_at] // parts).reshape((-1,) + (1,) * (len(extent) - axis_at - 1))

    gain = one(*cuts[0])
    for cut in cuts[1:]:
        gain = gain * one(*cut)
    return gain


def noise(stream_key, extent, scale, reach, kind=jnp.bfloat16):
    result = scale * jax.random.normal(stream_key, extent, jnp.float32)
    return jnp.clip(result, min=-reach, max=reach).astype(kind)


def setup_inputs(seed: int = 0) -> dict:
    splits = jax.random.split(jax.random.key(seed), 7)
    state = draw_state(jax.random.fold_in(splits[6], 71), 0)
    sponge_level = with_ends(jax.random.randint(splits[1], (NX, NT, NR), 0, 4), jax.random.fold_in(splits[1], 1), 0, 3).astype(jnp.int32)
    inv_dx = jnp.clip(jnp.exp(math.log(8.0) - 2.0794415 * jax.random.uniform(splits[2], (NX,), jnp.float32) ** steps_of(splits[2], (NX,), ((0, 16),), -0.2, 0.2)), 1.0, 8.0)
    inv_dr = jnp.clip(jnp.exp(jax.random.uniform(splits[3], (NR,), jnp.float32, math.log(1.0), math.log(8.0))), 1.0, 8.0)
    target = noise(splits[4], (5, NR), 1.0, 4.0, jnp.float32)
    cutoff = draw_cutoff(jax.random.fold_in(splits[6], 71), 0)
    return {"state": state, "sponge_level": sponge_level, "inv_dx": inv_dx, "inv_dr": inv_dr, "target": target, "cutoff": cutoff}


gas_factor = 0.4
time_step = 0.02
sponge_rate = 4.0


def cycle_radius(length):
    return 1.0 + 4.0 * jnp.arange(length, dtype=jnp.float32) / length


def flux_parts(fields, radius):
    density = fields[0]
    axial_momentum = fields[1]
    radial_momentum = fields[2]
    swirl_momentum = fields[3]
    energy = fields[4]
    axial_speed = axial_momentum / density
    radial_speed = radial_momentum / density
    swirl_speed = swirl_momentum / density
    pressure = gas_factor * (energy - 0.5 * (axial_momentum * axial_speed + radial_momentum * radial_speed + swirl_momentum * swirl_speed))
    enthalpy = energy + pressure
    axial_flux = jnp.stack([axial_momentum, axial_momentum * axial_speed + pressure, radial_momentum * axial_speed, swirl_momentum * axial_speed, enthalpy * axial_speed])
    radial_flux = radius * jnp.stack([radial_momentum, axial_momentum * radial_speed, radial_momentum * radial_speed + pressure, swirl_momentum * radial_speed, enthalpy * radial_speed])
    swirl_flux = jnp.stack([swirl_momentum, axial_momentum * swirl_speed, radial_momentum * swirl_speed, swirl_momentum * swirl_speed + pressure, enthalpy * swirl_speed])
    press_source = (pressure + swirl_momentum * swirl_speed) / radius
    turn_source = -(radial_momentum * swirl_speed) / radius
    return axial_flux, radial_flux, swirl_flux, press_source, turn_source


def reference(state, sponge_level, inv_dx, inv_dr, target, cutoff):
    block_total = NX // PL_DEV
    radius = cycle_radius(NR)
    mode_index = jnp.arange(NT // 2 + 1, dtype=jnp.int32)
    kept_modes = (mode_index[:, None] <= cutoff[None, :]).astype(jnp.float32)

    def one_block(block_index):
        offset = block_index * PL_DEV
        plane_index = offset - 1 + jnp.arange(PL_DEV + 2, dtype=jnp.int32)
        inside_grid = (plane_index >= 0) & (plane_index < NX)
        clipped = jnp.clip(plane_index, 0, NX - 1).astype(jnp.int32)
        slab_state = jnp.take(state, clipped, axis=1)
        axial_flux, radial_flux, swirl_flux, press_source, turn_source = flux_parts(slab_state, radius)
        axial_flux = jnp.where(inside_grid[None, :, None, None], axial_flux, 0.0)
        own_state = slab_state[:, 1:-1]
        radial_flux = radial_flux[:, 1:-1]
        swirl_flux = swirl_flux[:, 1:-1]
        press_source = press_source[1:-1]
        turn_source = turn_source[1:-1]
        scale_x = lax.dynamic_slice_in_dim(inv_dx, offset.astype(jnp.int32), PL_DEV, 0)
        levels = lax.dynamic_slice_in_dim(sponge_level, offset.astype(jnp.int32), PL_DEV, 0)
        axial_term = (axial_flux[:, 2:] - axial_flux[:, :-2]) * (0.5 * scale_x)[None, :, None, None]
        radial_pad = jnp.pad(radial_flux, ((0, 0), (0, 0), (0, 0), (1, 1)))
        radial_term = (radial_pad[..., 2:] - radial_pad[..., :-2]) * (0.5 * inv_dr / radius)
        swirl_term = (jnp.roll(swirl_flux, -1, axis=2) - jnp.roll(swirl_flux, 1, axis=2)) * ((NT / (4.0 * jnp.pi)) / radius)
        tendency = -(axial_term + radial_term + swirl_term)
        zero_field = jnp.zeros_like(press_source)
        tendency = tendency + jnp.stack([zero_field, zero_field, press_source, turn_source, zero_field])
        tendency = tendency - sponge_rate * levels.astype(jnp.float32)[None] * (own_state - target[:, None, None, :])
        updated = own_state + time_step * tendency
        inner_block = updated[..., :CYCLE]
        spectrum = jnp.fft.rfft(inner_block, axis=2)
        filtered = jnp.fft.irfft(spectrum * kept_modes[None, None], n=NT, axis=2).astype(updated.dtype)
        return jnp.concatenate([filtered, updated[..., CYCLE:]], axis=3)

    blocks = lax.map(one_block, jnp.arange(block_total, dtype=jnp.int32))
    return jnp.moveaxis(blocks, 0, 1).reshape(5, NX, NT, NR)
```

```python
import functools
import math

import jax
import jax.numpy as jnp
import ml_dtypes
import numpy as np
from jax import lax
from jax.experimental import pallas as pl
from jax.experimental.pallas import tpu as pltpu
from jax.sharding import PartitionSpec as P

CYCLE = 32
LANES = 128
PACK = LANES // CYCLE

gas_factor = 0.4
time_step = 0.02
sponge_rate = 4.0

VMEM_LIMIT = 56 * 1024 * 1024


def params(steps=1):
    return pltpu.CompilerParams(
        dimension_semantics=("arbitrary",) * steps, vmem_limit_bytes=VMEM_LIMIT
    )


def reciprocal(x):
    guess = pl.reciprocal(x, approx=True)
    return guess * (2.0 - x * guess)


def products(q):
    density, m, n, s, energy = q
    inverse = reciprocal(density)
    u, v, w = m * inverse, n * inverse, s * inverse
    mu, nv, sw = m * u, n * v, s * w
    pressure = gas_factor * energy - (0.5 * gas_factor) * (mu + nv + sw)
    return u, v, w, mu, nv, sw, pressure, energy + pressure


def axial_flux(q):
    u, _, _, mu, _, _, pressure, enthalpy = products(q)
    return (q[1], mu + pressure, q[2] * u, q[3] * u, enthalpy * u)


def swirl_flux(q):
    _, _, w, _, _, sw, pressure, enthalpy = products(q)
    return (q[3], q[1] * w, q[2] * w, sw + pressure, enthalpy * w)


def all_fluxes(q):
    u, v, w, mu, nv, sw, pressure, enthalpy = products(q)
    mv, mw, nw = q[1] * v, q[1] * w, q[2] * w
    axial = (q[1], mu + pressure, mv, mw, enthalpy * u)
    radial = (q[2], mv, nv + pressure, nw, enthalpy * v)
    swirl = (q[3], mw, nw, sw + pressure, enthalpy * w)
    return axial, radial, swirl


def fill_rows(rows_ref, inv_dr, cycles, columns):
    width = rows_ref.shape[-1]
    cycle = lax.broadcasted_iota(jnp.int32, (8, width), 1)
    spacing = 4.0 / cycles
    radius = 1.0 + spacing * cycle.astype(jnp.float32)
    inverse = 1.0 / radius
    half = (0.5 * time_step) * jnp.broadcast_to(inv_dr, (8, width)) * inverse
    rows_ref[0] = jnp.where(cycle == cycles - 1, 0.0, half * (radius + spacing))
    rows_ref[1] = jnp.where(cycle == 0, 0.0, half * (radius - spacing))
    rows_ref[2] = (time_step * columns / (4.0 * math.pi)) * inverse


def base_update(q, level, target, factors, radial, swirl, columns):
    up, down, around = factors
    width = q[0].shape[-1]
    sponge = level.astype(jnp.float32) * (time_step * sponge_rate)
    scaled = [around * flux for flux in swirl]
    source = 4.0 * math.pi / columns
    result = []
    for f in range(5):
        ahead = pltpu.roll(radial[f], width - 1, 1)
        behind = pltpu.roll(radial[f], 1, 1)
        value = q[f] - sponge * (q[f] - target[f]) - (up * ahead - down * behind)
        if f == 2:
            value = value + source * scaled[3]
        if f == 3:
            value = value - source * scaled[2]
        result.append(value)
    return result, scaled


def outer_kernel(odd_ref, state_ref, flux_ref, packed_ref):
    block = pl.program_id(0)
    flux = axial_flux([state_ref[f, 0] for f in range(5)])
    lane = lax.broadcasted_iota(jnp.int32, packed_ref.shape[1:], 1)
    for f in range(5):
        flux_ref[f] = flux[f]
        turned = pltpu.roll(flux[f][:, :LANES], block * CYCLE, 1)
        packed_ref[f] = jnp.where(lane // CYCLE == block, turned, packed_ref[f])


def outer_plane(odd, state):
    _, planes, columns, cycles = state.shape
    rows = columns // PACK
    return pl.pallas_call(
        outer_kernel,
        grid_spec=pltpu.PrefetchScalarGridSpec(
            num_scalar_prefetch=1,
            grid=(PACK,),
            in_specs=[pl.BlockSpec((5, 1, rows, cycles), lambda b, odd: (0, odd[0] * (planes - 1), b, 0))],
            out_specs=[
                pl.BlockSpec((5, rows, cycles), lambda b, odd: (0, b, 0)),
                pl.BlockSpec((5, rows, LANES), lambda b, odd: (0, 0, 0)),
            ],
        ),
        out_shape=[
            jax.ShapeDtypeStruct((5, columns, cycles), jnp.float32),
            jax.ShapeDtypeStruct((5, rows, LANES), jnp.float32),
        ],
        compiler_params=params(),
        name="outer_plane",
    )(odd, state)


def inner_kernel(odd_ref, state_ref, first_ref, last_ref, flux_ref, edge_ref):
    flux = axial_flux([state_ref[f, 0] for f in range(5)])
    for f in range(5):
        flux_ref[f] = flux[f]
    low = swirl_flux([last_ref[f, :, 7, :] for f in range(5)])
    high = swirl_flux([first_ref[f, :, 0, :] for f in range(5)])
    for f in range(5):
        edge_ref[0, f] = low[f]
        edge_ref[1, f] = high[f]


def inner_plane(odd, state):
    _, planes, columns, cycles = state.shape
    steps = planes // 8
    rows = columns // steps
    return pl.pallas_call(
        inner_kernel,
        grid_spec=pltpu.PrefetchScalarGridSpec(
            num_scalar_prefetch=1,
            grid=(steps,),
            in_specs=[
                pl.BlockSpec((5, 1, rows, cycles), lambda b, odd: (0, (1 - odd[0]) * (planes - 1), b, 0)),
                pl.BlockSpec((5, 8, 8, cycles), lambda b, odd: (0, b, 0, 0)),
                pl.BlockSpec((5, 8, 8, cycles), lambda b, odd: (0, b, columns // 8 - 1, 0)),
            ],
            out_specs=[
                pl.BlockSpec((5, rows, cycles), lambda b, odd: (0, b, 0)),
                pl.BlockSpec((2, 5, 8, cycles), lambda b, odd: (0, 0, b, 0)),
            ],
        ),
        out_shape=[
            jax.ShapeDtypeStruct((5, columns, cycles), jnp.float32),
            jax.ShapeDtypeStruct((2, 5, planes, cycles), jnp.float32),
        ],
        compiler_params=params(),
        name="inner_plane",
    )(odd, state, state, state)


def modes_kernel(
    odd_ref, scale_ref, state_ref, before_ref, after_ref, level_ref, inv_dr_ref, target_ref, near_ref, far_ref,
    table_ref, edge_ref, out_ref, rows_ref, axial_ref, swirl_ref, base_ref, split_ref, total_ref,
    *, cycles, cells, chunk,
):
    step = pl.program_id(0)
    steps = pl.num_programs(0)
    columns = state_ref.shape[2]
    odd = odd_ref[0]
    far_rows = far_ref.shape[1]

    @pl.when(step == 0)
    def _():
        fill_rows(rows_ref, inv_dr_ref[...], cycles, cells)
        for f in range(5):
            for i in range(PACK):
                swirl_ref[i, f, 0:8] = jnp.zeros((8, LANES), jnp.float32)
                swirl_ref[i, f, columns + 8 : columns + 16] = jnp.zeros((8, LANES), jnp.float32)

    def load(ref, plane, start):
        return [ref[f, plane, pl.ds(start, chunk), :] for f in range(5)]

    def halo(slot, use_near):
        for f in range(5):
            for b in range(PACK):
                away = far_ref[f]
                away = away if b == 0 else pltpu.roll(away, LANES - b * CYCLE, 1)
                near = near_ref[f, b * far_rows : (b + 1) * far_rows]
                axial_ref[slot, f, b * far_rows : (b + 1) * far_rows] = jnp.where(use_near, near, away)

    def neighbour(slot, ref):
        def one(c, _):
            start = pl.multiple_of(c * chunk, chunk)
            flux = axial_flux(load(ref, 0, start))
            for f in range(5):
                axial_ref[slot, f, pl.ds(start, chunk)] = flux[f]
            return 0

        lax.fori_loop(0, columns // chunk, one, 0)

    pl.when(step == 0)(lambda: halo(0, odd == 1))
    pl.when(step > 0)(lambda: neighbour(0, before_ref))
    pl.when(step == steps - 1)(lambda: halo(PACK + 1, odd == 0))
    pl.when(step < steps - 1)(lambda: neighbour(PACK + 1, after_ref))

    def wide(rows):
        return jnp.broadcast_to(rows[None], (chunk // 8, 8, LANES)).reshape(chunk, LANES)

    def first(c, _):
        start = pl.multiple_of(c * chunk, chunk)
        factors = [wide(rows_ref[k]) for k in range(3)]
        target = [jnp.broadcast_to(target_ref[f : f + 1], (chunk, LANES)) for f in range(5)]
        for i in range(PACK):
            q = load(state_ref, i, start)
            axial, radial, swirl = all_fluxes(q)
            level = level_ref[i, pl.ds(start, chunk), :]
            base, scaled = base_update(q, level, target, factors, radial, swirl, cells)
            for f in range(5):
                axial_ref[i + 1, f, pl.ds(start, chunk)] = axial[f]
                swirl_ref[i, f, pl.ds(start + 8, chunk)] = scaled[f]
                base_ref[i, f, pl.ds(start, chunk)] = base[f]
        return 0

    lax.fori_loop(0, columns // chunk, first, 0)

    lane = lax.broadcasted_iota(jnp.int32, (chunk, LANES), 1)

    def packed(parts, rows):
        result = parts[0]
        for i in range(1, PACK):
            result = jnp.where(lane[:rows] // CYCLE == i, pltpu.roll(parts[i], i * CYCLE, 1), result)
        return result

    factor = [(0.5 * time_step) * scale_ref[step * PACK + i] for i in range(PACK)]
    for f in range(5):
        total = jnp.zeros((8, LANES), jnp.float32)
        for c in range(columns // chunk):
            start = c * chunk
            parts = []
            for i in range(PACK):
                value = base_ref[i, f, start : start + chunk]
                value = value - factor[i] * (
                    axial_ref[i + 2, f, start : start + chunk] - axial_ref[i, f, start : start + chunk]
                )
                value = value + (
                    swirl_ref[i, f, start + 7 : start + 7 + chunk] - swirl_ref[i, f, start + 9 : start + 9 + chunk]
                )
                parts.append(value)
            value = packed(parts, chunk)
            high = value.astype(jnp.bfloat16)
            split_ref[f, start : start + chunk] = high
            split_ref[f, columns + start : columns + start + chunk] = (value - high.astype(jnp.float32)).astype(
                jnp.bfloat16
            )
            total = total + value.reshape(chunk // 8, 8, LANES).sum(axis=0)
        sums = jnp.dot(table_ref[...], split_ref[f], preferred_element_type=jnp.float32)
        half = sums.shape[0] // 2
        start_row = packed([swirl_ref[i, f, 8:16] for i in range(PACK)], 8)[0:1]
        end_row = packed([swirl_ref[i, f, columns : columns + 8] for i in range(PACK)], 8)[7:8]
        group = step * 5 + f
        out_ref[pl.ds(pl.multiple_of(group * half, half), half), :] = (
            sums[:half] + sums[half:] + (edge_ref[1] * end_row - edge_ref[0] * start_row)
        )
        mean = total.sum(axis=0, keepdims=True) + (end_row - start_row)
        out_ref[pl.ds(steps * 5 * half + group, 1), :] = mean


def mode_rows(planes, half):
    groups = 5 * planes // PACK
    return groups * half + -(-groups // 8) * 8


def inner_modes(odd, scale, state, sponge, inv_dr, target, near, far, table, edge, cells):
    _, planes, columns, cycles = state.shape
    half = table.shape[0] // 2
    chunk = min(32, columns)
    rows = mode_rows(planes, half)
    whole = lambda *shape: pl.BlockSpec(shape, lambda g, odd: (0,) * len(shape))
    return pl.pallas_call(
        functools.partial(modes_kernel, cycles=cycles, cells=cells, chunk=chunk),
        grid_spec=pltpu.PrefetchScalarGridSpec(
            num_scalar_prefetch=1,
            grid=(planes // PACK,),
            in_specs=[
                pl.BlockSpec(memory_space=pltpu.SMEM),
                pl.BlockSpec((5, PACK, columns, LANES), lambda g, odd: (0, g, 0, 0)),
                pl.BlockSpec((5, 1, columns, LANES), lambda g, odd: (0, jnp.maximum(g * PACK - 1, 0), 0, 0)),
                pl.BlockSpec(
                    (5, 1, columns, LANES), lambda g, odd: (0, jnp.minimum(g * PACK + PACK, planes - 1), 0, 0)
                ),
                pl.BlockSpec((PACK, columns, LANES), lambda g, odd: (g, 0, 0)),
                whole(1, LANES),
                whole(5, LANES),
                whole(5, columns, LANES),
                whole(5, columns // PACK, LANES),
                whole(*table.shape),
                whole(*edge.shape),
            ],
            out_specs=whole(rows, LANES),
            scratch_shapes=[
                pltpu.VMEM((3, 8, LANES), jnp.float32),
                pltpu.VMEM((PACK + 2, 5, columns, LANES), jnp.float32),
                pltpu.VMEM((PACK, 5, columns + 16, LANES), jnp.float32),
                pltpu.VMEM((PACK, 5, columns, LANES), jnp.float32),
                pltpu.VMEM((5, 2 * columns, LANES), jnp.bfloat16),
                pltpu.VMEM((8, LANES), jnp.float32),
            ],
        ),
        out_shape=jax.ShapeDtypeStruct((rows, LANES), jnp.float32),
        compiler_params=params(),
        name="inner_modes",
    )(odd, scale, state, state, state, sponge, inv_dr, target, near, far, table, edge)


def update_kernel(
    odd_ref, scale_ref, state_ref, level_ref, inv_dr_ref, target_ref, near_ref, halo_ref, out_ref,
    rows_ref, axial_ref, swirl_ref, base_ref, *, cells, chunk,
):
    step = pl.program_id(0)
    planes = pl.num_programs(0) - 1
    columns, cycles = state_ref.shape[2:]
    tiles = cycles // LANES
    odd = odd_ref[0]

    @pl.when(step == 0)
    def _():
        fill_rows(rows_ref, inv_dr_ref[...], cycles, cells)

    def lanes(value, tile):
        return value[:, tile * LANES : (tile + 1) * LANES]

    def finish(c, axial_of):
        start = pl.multiple_of(c * chunk, chunk)
        factor = (0.5 * time_step) * scale_ref[step - 1]
        parity = lax.rem(step + 1, 2)
        for f in range(5):
            ahead = factor * axial_of(f)
            for tile in range(tiles):
                value = lanes(base_ref[f, pl.ds(start, chunk), :], tile) - lanes(ahead, tile)
                value = value + (
                    swirl_ref[parity, f, tile, pl.ds(start + 7, chunk)]
                    - swirl_ref[parity, f, tile, pl.ds(start + 9, chunk)]
                )
                out_ref[f, 0, pl.ds(start, chunk), tile * LANES : (tile + 1) * LANES] = value

    def compute(c, beginning):
        start = pl.multiple_of(c * chunk, chunk)
        q = [state_ref[f, 0, pl.ds(start, chunk), :] for f in range(5)]
        axial, radial, swirl = all_fluxes(q)
        if not beginning:
            finish(c, lambda f: axial[f])
        factor = (0.5 * time_step) * scale_ref[step]
        target = [jnp.broadcast_to(target_ref[f : f + 1], (chunk, cycles)) for f in range(5)]
        base, scaled = base_update(
            q, level_ref[0, pl.ds(start, chunk), :], target, [rows_ref[k] for k in range(3)], radial, swirl, cells
        )
        parity = lax.rem(step, 2)
        for f in range(5):
            if beginning:
                behind = jnp.where(odd == 1, near_ref[f, pl.ds(start, chunk), :], 0.0)
            else:
                behind = axial_ref[f, pl.ds(start, chunk), :]
            base_ref[f, pl.ds(start, chunk), :] = base[f] + factor * behind
            axial_ref[f, pl.ds(start, chunk), :] = axial[f]
            for tile in range(tiles):
                swirl_ref[parity, f, tile, pl.ds(start + 8, chunk)] = lanes(scaled[f], tile)
        return 0

    @pl.when(step < planes)
    def _():
        parity = lax.rem(step, 2)
        around = rows_ref[2][0:1]
        for f in range(5):
            low = around * halo_ref[0, f, pl.ds(step, 1), :]
            high = around * halo_ref[1, f, pl.ds(step, 1), :]
            for tile in range(tiles):
                swirl_ref[parity, f, tile, 7:8] = lanes(low, tile)
                swirl_ref[parity, f, tile, columns + 8 : columns + 9] = lanes(high, tile)

    count = columns // chunk

    def loop(body):
        lax.fori_loop(0, count, body, 0)

    pl.when(step == 0)(lambda: loop(lambda c, _: compute(c, True)))
    pl.when(jnp.logical_and(step > 0, step < planes))(lambda: loop(lambda c, _: compute(c, False)))

    def last(c, _):
        start = pl.multiple_of(c * chunk, chunk)
        finish(c, lambda f: jnp.where(odd == 0, near_ref[f, pl.ds(start, chunk), :], 0.0))
        return 0

    pl.when(step == planes)(lambda: loop(last))


def bulk_update(odd, scale, state, sponge, inv_dr, target, near, halo, cells):
    _, planes, columns, cycles = state.shape
    whole = lambda *shape: pl.BlockSpec(shape, lambda g, odd: (0,) * len(shape))
    return pl.pallas_call(
        functools.partial(update_kernel, cells=cells, chunk=8),
        grid_spec=pltpu.PrefetchScalarGridSpec(
            num_scalar_prefetch=1,
            grid=(planes + 1,),
            in_specs=[
                pl.BlockSpec(memory_space=pltpu.SMEM),
                pl.BlockSpec((5, 1, columns, cycles), lambda g, odd: (0, jnp.minimum(g, planes - 1), 0, 0)),
                pl.BlockSpec((1, columns, cycles), lambda g, odd: (jnp.minimum(g, planes - 1), 0, 0)),
                whole(1, cycles),
                whole(5, cycles),
                whole(5, columns, cycles),
                whole(2, 5, planes, cycles),
            ],
            out_specs=pl.BlockSpec((5, 1, columns, cycles), lambda g, odd: (0, jnp.maximum(g - 1, 0), 0, 0)),
            scratch_shapes=[
                pltpu.VMEM((3, 8, cycles), jnp.float32),
                pltpu.VMEM((5, columns, cycles), jnp.float32),
                pltpu.VMEM((2, 5, cycles // LANES, columns + 16, LANES), jnp.float32),
                pltpu.VMEM((5, columns, cycles), jnp.float32),
            ],
        ),
        out_shape=jax.ShapeDtypeStruct(state.shape, jnp.float32),
        compiler_params=params(),
        name="bulk_update",
    )(odd, scale, state, sponge, inv_dr, target, near, halo)


def filter_kernel(cutoff_ref, table_ref, *refs, cells):
    *sums, state_ref, out_ref, split_ref = refs
    step = pl.program_id(0)
    steps = pl.num_programs(0)
    half = table_ref.shape[1] // 4
    count = half // 2
    columns = out_ref.shape[2]
    mode = lax.broadcasted_iota(jnp.int32, (half, LANES), 0)
    mode = jnp.where(mode >= count, mode - count, mode) + 1
    weight = jnp.where(mode <= cutoff_ref[...], 2.0 / cells, 0.0)
    lane = lax.broadcasted_iota(jnp.int32, (columns, LANES), 1)
    for f in range(5):
        group = step * 5 + f
        rows = pl.ds(pl.multiple_of(group * half, half), half)
        coefficient = sums[0][rows, :]
        mean = sums[0][pl.ds(steps * 5 * half + group, 1), :]
        for other in sums[1:]:
            coefficient = coefficient + other[rows, :]
            mean = mean + other[pl.ds(steps * 5 * half + group, 1), :]
        coefficient = coefficient * weight
        high = coefficient.astype(jnp.bfloat16)
        low = (coefficient - high.astype(jnp.float32)).astype(jnp.bfloat16)
        for k in range(2):
            split_ref[f, 2 * k * half : (2 * k + 1) * half] = high
            split_ref[f, (2 * k + 1) * half : (2 * k + 2) * half] = low
        values = jnp.dot(table_ref[...], split_ref[f], preferred_element_type=jnp.float32) + mean * (1.0 / cells)
        for i in range(PACK):
            turned = values if i == 0 else pltpu.roll(values, LANES - i * CYCLE, 1)
            out_ref[f, i] = jnp.where(lane < CYCLE, turned, state_ref[f, i])


def put_filtered(cutoff, table, sums, updated, cells):
    _, planes, columns, cycles = updated.shape
    whole = lambda *shape: pl.BlockSpec(shape, lambda g: (0,) * len(shape))
    block = pl.BlockSpec((5, PACK, columns, LANES), lambda g: (0, g, 0, 0))
    return pl.pallas_call(
        functools.partial(filter_kernel, cells=cells),
        grid=(planes // PACK,),
        in_specs=[whole(1, LANES), whole(*table.shape)] + [whole(*part.shape) for part in sums] + [block],
        out_specs=block,
        scratch_shapes=[pltpu.VMEM((5, table.shape[1], LANES), jnp.bfloat16)],
        out_shape=jax.ShapeDtypeStruct(updated.shape, jnp.float32),
        input_output_aliases={2 + len(sums): 0},
        compiler_params=params(),
        name="put_filtered",
    )(cutoff, table, *sums, updated)


def finish_kernel(odd_ref, scale_ref, flux_ref, state_ref, out_ref):
    odd = odd_ref[0]
    planes = scale_ref.shape[0]
    factor = (0.5 * time_step) * scale_ref[odd * (planes - 1)]
    factor = jnp.where(odd == 1, -factor, factor)
    lane = lax.broadcasted_iota(jnp.int32, out_ref.shape[2:], 1)
    for f in range(5):
        out_ref[f, 0] = state_ref[f, 0] + jnp.where(lane < CYCLE, 0.0, factor * flux_ref[f])


def finish_plane(odd, scale, flux, updated):
    _, planes, columns, cycles = updated.shape
    rows = columns // 4
    block = pl.BlockSpec((5, 1, rows, cycles), lambda b, odd: (0, odd[0] * (planes - 1), b, 0))
    return pl.pallas_call(
        finish_kernel,
        grid_spec=pltpu.PrefetchScalarGridSpec(
            num_scalar_prefetch=1,
            grid=(4,),
            in_specs=[
                pl.BlockSpec(memory_space=pltpu.SMEM),
                pl.BlockSpec((5, rows, cycles), lambda b, odd: (0, b, 0)),
                block,
            ],
            out_specs=block,
        ),
        out_shape=jax.ShapeDtypeStruct(updated.shape, jnp.float32),
        input_output_aliases={3: 0},
        compiler_params=params(),
        name="finish_plane",
    )(odd, scale, flux, updated)


def mode_tables(cells, sectors):
    columns = cells // sectors
    mode = np.arange(1, cells // 8 + 1)

    def waves(cell):
        angle = 2.0 * np.pi / cells * ((mode[:, None] * cell[None, :]) % cells)
        return np.concatenate([np.cos(angle), np.sin(angle)])

    forward, inverse, edge = [], [], []
    for sector in range(sectors):
        wave = waves(sector * columns + np.arange(columns))
        high = wave.astype(ml_dtypes.bfloat16)
        low = (wave - high.astype(np.float64)).astype(ml_dtypes.bfloat16)
        forward.append(np.block([[high, high], [low, low]]))
        inverse.append(np.concatenate([high.T, high.T, low.T, low.T], axis=1))
        ends = waves(np.array([sector * columns - 1, (sector + 1) * columns]) % cells)
        edge.append(np.broadcast_to(ends.T[:, :, None], (2, ends.shape[0], LANES)))
    return np.stack(forward), np.stack(inverse), np.stack(edge).astype(np.float32)


def body(forward, inverse, edge, cells, state, sponge_level, inv_dx, inv_dr, target, cutoff):
    sectors = lax.axis_size("az")
    rows = lax.axis_size("gx")
    sector = lax.axis_index("az")
    odd = jnp.reshape(lax.rem(lax.axis_index("gx"), 2), (1,)).astype(jnp.int32)
    cycles = state.shape[3]
    inv_dr = inv_dr.reshape(1, cycles)
    cutoff = jnp.tile(cutoff, PACK).reshape(1, LANES)
    pick = lambda table: lax.dynamic_index_in_dim(table, sector, 0, False)

    near_pairs = [(i ^ 1, i) for i in range(rows) if i ^ 1 < rows]
    far_pairs = [(i, i + 1) for i in range(1, rows - 1, 2)] + [(i + 1, i) for i in range(1, rows - 1, 2)]
    shifted = lambda part, by: lax.ppermute(part, "az", [(i, (i + by) % sectors) for i in range(sectors)])

    far_flux, far_packed = outer_plane(odd, state)
    far_packed = lax.ppermute(far_packed, "gx", far_pairs)
    far_flux = lax.ppermute(far_flux, "gx", far_pairs)
    near_flux, edges = inner_plane(odd, state)
    near_flux = lax.ppermute(near_flux, "gx", near_pairs)
    if sectors == 2:
        halo = shifted(edges, 1)
    else:
        halo = jnp.stack([shifted(edges[0], 1), shifted(edges[1], sectors - 1)])
    sums = inner_modes(
        odd, inv_dx, state, sponge_level, inv_dr, target, near_flux, far_packed, pick(forward), pick(edge), cells
    )
    others = [shifted(sums, by) for by in range(1, sectors)]
    updated = bulk_update(odd, inv_dx, state, sponge_level, inv_dr, target, near_flux, halo, cells)
    updated = put_filtered(cutoff, pick(inverse), [sums, *others], updated, cells)
    return finish_plane(odd, inv_dx, far_flux, updated)


def solution(mesh):
    def whole(state, sponge_level, inv_dx, inv_dr, target, cutoff):
        cells = state.shape[2]
        tables = mode_tables(cells, mesh.shape["az"])
        mapped = jax.shard_map(
            functools.partial(body, *(jnp.asarray(table) for table in tables), cells),
            mesh=mesh,
            in_specs=(P(None, "gx", "az", None), P("gx", "az", None), P("gx"), P(), P(), P()),
            out_specs=P(None, "gx", "az", None),
            check_vma=False,
        )
        return mapped(state, sponge_level, inv_dx, inv_dr, target, cutoff)

    return whole
```

```python
import functools
import math

import jax
import jax.numpy as jnp
import ml_dtypes
import numpy as np
from jax import lax
from jax.experimental import pallas as pl
from jax.experimental.pallas import tpu as pltpu
from jax.sharding import PartitionSpec as P

CYCLE = 32
LANES = 128
PACK = LANES // CYCLE

gas_factor = 0.4
time_step = 0.02
sponge_rate = 4.0

MIB = 1024 * 1024


def params(steps, limit):
    return pltpu.CompilerParams(
        dimension_semantics=("arbitrary",) * steps, vmem_limit_bytes=limit * MIB
    )


def resident(x):
    return pltpu.with_memory_space_constraint(x, pltpu.VMEM)


VMEM_SPEC = pl.BlockSpec(memory_space=pltpu.VMEM)
SMEM_SPEC = pl.BlockSpec(memory_space=pltpu.SMEM)
HBM_SPEC = pl.BlockSpec(memory_space=pl.ANY)


def products(q):
    density, m, n, s, energy = q
    inverse = pltpu.reciprocal(density, approx=True)
    u, v, w = m * inverse, n * inverse, s * inverse
    mu, nv, sw = m * u, n * v, s * w
    pressure = gas_factor * energy - (0.5 * gas_factor) * (mu + nv + sw)
    return u, v, w, mu, nv, sw, pressure, energy + pressure


def axial_flux(q):
    u, _, _, mu, _, _, pressure, enthalpy = products(q)
    return (q[1], mu + pressure, q[2] * u, q[3] * u, enthalpy * u)


def swirl_flux(q):
    _, _, w, _, _, sw, pressure, enthalpy = products(q)
    return (q[3], q[1] * w, q[2] * w, sw + pressure, enthalpy * w)


def all_fluxes(q):
    u, v, w, mu, nv, sw, pressure, enthalpy = products(q)
    mv, mw, nw = q[1] * v, q[1] * w, q[2] * w
    axial = (q[1], mu + pressure, mv, mw, enthalpy * u)
    radial = (q[2], mv, nv + pressure, nw, enthalpy * v)
    swirl = (q[3], mw, nw, sw + pressure, enthalpy * w)
    return axial, radial, swirl


def fill_rows(rows_ref, inv_dr, start, cycles, cells):
    width = rows_ref.shape[-1]
    cycle = lax.broadcasted_iota(jnp.int32, (8, width), 1) + start
    spacing = 4.0 / cycles
    radius = 1.0 + spacing * cycle.astype(jnp.float32)
    inverse = 1.0 / radius
    half = (0.5 * time_step) * jnp.broadcast_to(inv_dr, (8, width)) * inverse
    rows_ref[0] = jnp.where(cycle == start + width - 1, 0.0, half * (radius + spacing))
    rows_ref[1] = jnp.where(cycle == 0, 0.0, half * (radius - spacing))
    rows_ref[2] = (time_step * cells / (4.0 * math.pi)) * inverse


def base_update(q, sponge, target, ahead, behind, up, down, scaled, cells):
    source = 4.0 * math.pi / cells
    result = []
    for f in range(5):
        value = q[f] - sponge * (q[f] - target[f]) - (up * ahead[f] - down * behind[f])
        if f == 2:
            value = value + source * scaled[3]
        if f == 3:
            value = value - source * scaled[2]
        result.append(value)
    return result


def outer_kernel(odd_ref, state_ref, flux_ref, packed_ref):
    step = pl.program_id(0)
    rows = packed_ref.shape[1]
    blocks = state_ref.shape[2] // rows
    flux = axial_flux([state_ref[f, 0] for f in range(5)])
    lane = lax.broadcasted_iota(jnp.int32, packed_ref.shape[1:], 1)
    for f in range(5):
        flux_ref[f, pl.ds(pl.multiple_of(step * state_ref.shape[2], 8), state_ref.shape[2])] = flux[f]
        for i in range(blocks):
            block = step * blocks + i
            turned = pltpu.roll(flux[f][i * rows : (i + 1) * rows, :LANES], block * CYCLE, 1)
            packed_ref[f] = jnp.where(lane // CYCLE == block, turned, packed_ref[f])


def outer_plane(odd, state):
    _, planes, columns, cycles = state.shape
    steps = 2
    return pl.pallas_call(
        outer_kernel,
        grid_spec=pltpu.PrefetchScalarGridSpec(
            num_scalar_prefetch=1,
            grid=(steps,),
            in_specs=[
                pl.BlockSpec((5, 1, columns // steps, cycles), lambda b, odd: (0, odd[0] * (planes - 1), b, 0))
            ],
            out_specs=[VMEM_SPEC, VMEM_SPEC],
        ),
        out_shape=[
            pltpu.VMEM((5, columns, cycles), jnp.float32),
            pltpu.VMEM((5, columns // PACK, LANES), jnp.float32),
        ],
        compiler_params=params(1, 8),
        name="outer_plane",
    )(odd, state)


def inner_kernel(odd_ref, state_ref, first_ref, last_ref, flux_ref, edge_ref):
    step = pl.program_id(0)
    rows = state_ref.shape[2]
    flux = axial_flux([state_ref[f, 0] for f in range(5)])
    for f in range(5):
        flux_ref[f, pl.ds(pl.multiple_of(step * rows, 8), rows)] = flux[f]
    low = swirl_flux([last_ref[f, :, 7, :] for f in range(5)])
    high = swirl_flux([first_ref[f, :, 0, :] for f in range(5)])
    planes = pl.ds(pl.multiple_of(step * 8, 8), 8)
    for f in range(5):
        edge_ref[0, f, planes] = low[f]
        edge_ref[1, f, planes] = high[f]


def inner_plane(odd, state):
    _, planes, columns, cycles = state.shape
    steps = planes // 8
    return pl.pallas_call(
        inner_kernel,
        grid_spec=pltpu.PrefetchScalarGridSpec(
            num_scalar_prefetch=1,
            grid=(steps,),
            in_specs=[
                pl.BlockSpec((5, 1, columns // steps, cycles), lambda b, odd: (0, (1 - odd[0]) * (planes - 1), b, 0)),
                pl.BlockSpec((5, 8, 8, cycles), lambda b, odd: (0, b, 0, 0)),
                pl.BlockSpec((5, 8, 8, cycles), lambda b, odd: (0, b, columns // 8 - 1, 0)),
            ],
            out_specs=[VMEM_SPEC, VMEM_SPEC],
        ),
        out_shape=[
            pltpu.VMEM((5, columns, cycles), jnp.float32),
            pltpu.VMEM((2, 5, planes, cycles), jnp.float32),
        ],
        compiler_params=params(1, 12),
        name="inner_plane",
    )(odd, state, state, state)


def modes_kernel(
    place_ref, scale_ref, state_ref, before_ref, after_ref, level_ref, inv_dr_ref, target_ref, table_ref, edge_ref,
    near_ref, far_ref, sums_ref, tile_ref, behind_ref, rows_ref, axial_ref, swirl_ref, base_ref, split_ref,
    *, cycles, cells, chunk,
):
    step = pl.program_id(0)
    steps = pl.num_programs(0)
    columns = state_ref.shape[2]
    odd = place_ref[0]
    far_rows = far_ref.shape[1]

    @pl.when(step == 0)
    def _():
        fill_rows(rows_ref, inv_dr_ref[...], 0, cycles, cells)
        for f in range(5):
            for i in range(PACK):
                swirl_ref[i, f, 0:8] = jnp.zeros((8, LANES), jnp.float32)
                swirl_ref[i, f, columns + 8 : columns + 16] = jnp.zeros((8, LANES), jnp.float32)

    def load(ref, plane, start):
        return [ref[f, plane, pl.ds(start, chunk), :] for f in range(5)]

    def halo(slot, use_near):
        for f in range(5):
            for b in range(PACK):
                away = far_ref[f]
                away = away if b == 0 else pltpu.roll(away, LANES - b * CYCLE, 1)
                near = near_ref[f, b * far_rows : (b + 1) * far_rows, :LANES]
                axial_ref[slot, f, b * far_rows : (b + 1) * far_rows] = jnp.where(
                    use_near, near, jnp.where(lane[:far_rows] < CYCLE, away, 0.0)
                )

    def neighbour(slot, ref):
        def one(c, _):
            start = pl.multiple_of(c * chunk, chunk)
            flux = axial_flux(load(ref, 0, start))
            for f in range(5):
                axial_ref[slot, f, pl.ds(start, chunk)] = flux[f]
            return 0

        lax.fori_loop(0, columns // chunk, one, 0, unroll=True)

    lane = lax.broadcasted_iota(jnp.int32, (chunk, LANES), 1)
    pl.when(step == 0)(lambda: halo(0, odd == 1))
    pl.when(step > 0)(lambda: neighbour(0, before_ref))
    pl.when(step == steps - 1)(lambda: halo(PACK + 1, odd == 0))
    pl.when(step < steps - 1)(lambda: neighbour(PACK + 1, after_ref))

    def wide(row):
        return jnp.broadcast_to(row[None], (chunk // 8, 8, LANES)).reshape(chunk, LANES)

    def first(c, _):
        start = pl.multiple_of(c * chunk, chunk)
        up, down, around = [wide(rows_ref[k]) for k in range(3)]
        target = [jnp.broadcast_to(target_ref[f : f + 1], (chunk, LANES)) for f in range(5)]
        for i in range(PACK):
            q = load(state_ref, i, start)
            axial, radial, swirl = all_fluxes(q)
            sponge = level_ref[i, pl.ds(start, chunk), :].astype(jnp.float32) * (time_step * sponge_rate)
            scaled = [around * flux for flux in swirl]
            ahead = [pltpu.roll(flux, LANES - 1, 1) for flux in radial]
            behind = [pltpu.roll(flux, 1, 1) for flux in radial]
            base = base_update(q, sponge, target, ahead, behind, up, down, scaled, cells)
            plane = step * PACK + i
            for f in range(5):
                behind_ref[f, plane, pl.ds(start, chunk)] = behind[f]
                axial_ref[i + 1, f, pl.ds(start, chunk)] = axial[f]
                swirl_ref[i, f, pl.ds(start + 8, chunk)] = scaled[f]
                base_ref[i, f, pl.ds(start, chunk)] = base[f]
        return 0

    lax.fori_loop(0, columns // chunk, first, 0, unroll=True)

    def packed(parts, rows):
        result = parts[0]
        for i in range(1, PACK):
            result = jnp.where(lane[:rows] // CYCLE == i, pltpu.roll(parts[i], i * CYCLE, 1), result)
        return result

    factor = [(0.5 * time_step) * scale_ref[step * PACK + i] for i in range(PACK)]
    for f in range(5):
        total = jnp.zeros((8, LANES), jnp.float32)
        for c in range(columns // chunk):
            start = c * chunk
            parts = []
            for i in range(PACK):
                value = base_ref[i, f, start : start + chunk]
                value = value - factor[i] * (
                    axial_ref[i + 2, f, start : start + chunk] - axial_ref[i, f, start : start + chunk]
                )
                inside = value + (
                    swirl_ref[i, f, start + 7 : start + 7 + chunk] - swirl_ref[i, f, start + 9 : start + 9 + chunk]
                )
                tile_ref[f, step * PACK + i, start : start + chunk] = inside
                parts.append(inside)
            value = packed(parts, chunk)
            high = value.astype(jnp.bfloat16)
            split_ref[f, start : start + chunk] = high
            split_ref[f, columns + start : columns + start + chunk] = (value - high.astype(jnp.float32)).astype(
                jnp.bfloat16
            )
            total = total + value.reshape(chunk // 8, 8, LANES).sum(axis=0)
        sums = jnp.dot(table_ref[0], split_ref[f], preferred_element_type=jnp.float32)
        half = sums.shape[0] // 2
        start_row = packed([swirl_ref[i, f, 8:16] for i in range(PACK)], 8)[0:1]
        end_row = packed([swirl_ref[i, f, columns : columns + 8] for i in range(PACK)], 8)[7:8]
        group = step * 5 + f
        sums_ref[pl.ds(pl.multiple_of(group * half, half), half), :] = (
            sums[:half] + sums[half:] + (edge_ref[0, 1] * end_row - edge_ref[0, 0] * start_row)
        )
        mean = total.sum(axis=0, keepdims=True) + (end_row - start_row)
        sums_ref[pl.ds(steps * 5 * half + group, 1), :] = mean


def mode_rows(planes, half):
    groups = 5 * planes // PACK
    return groups * half + -(-groups // 8) * 8


def inner_modes(place, scale, state, sponge, inv_dr, target, table, edge, near, far, cells):
    _, planes, columns, cycles = state.shape
    half = table.shape[1] // 2
    chunk = min(32, columns)
    whole = lambda *shape: pl.BlockSpec(shape, lambda g, place: (0,) * len(shape))
    tile = pltpu.VMEM((5, planes, columns, LANES), jnp.float32)
    return pl.pallas_call(
        functools.partial(modes_kernel, cycles=cycles, cells=cells, chunk=chunk),
        grid_spec=pltpu.PrefetchScalarGridSpec(
            num_scalar_prefetch=1,
            grid=(planes // PACK,),
            in_specs=[
                SMEM_SPEC,
                pl.BlockSpec((5, PACK, columns, LANES), lambda g, place: (0, g, 0, 0)),
                pl.BlockSpec((5, 1, columns, LANES), lambda g, place: (0, jnp.maximum(g * PACK - 1, 0), 0, 0)),
                pl.BlockSpec(
                    (5, 1, columns, LANES), lambda g, place: (0, jnp.minimum(g * PACK + PACK, planes - 1), 0, 0)
                ),
                pl.BlockSpec((PACK, columns, LANES), lambda g, place: (g, 0, 0)),
                whole(1, LANES),
                whole(5, LANES),
                pl.BlockSpec((1,) + table.shape[1:], lambda g, place: (place[1], 0, 0)),
                pl.BlockSpec((1,) + edge.shape[1:], lambda g, place: (place[1], 0, 0, 0)),
                VMEM_SPEC,
                VMEM_SPEC,
            ],
            out_specs=[VMEM_SPEC, VMEM_SPEC, VMEM_SPEC],
            scratch_shapes=[
                pltpu.VMEM((3, 8, LANES), jnp.float32),
                pltpu.VMEM((PACK + 2, 5, columns, LANES), jnp.float32),
                pltpu.VMEM((PACK, 5, columns + 16, LANES), jnp.float32),
                pltpu.VMEM((PACK, 5, columns, LANES), jnp.float32),
                pltpu.VMEM((5, 2 * columns, LANES), jnp.bfloat16),
            ],
        ),
        out_shape=[pltpu.VMEM((mode_rows(planes, half), LANES), jnp.float32), tile, tile],
        compiler_params=params(1, 20),
        name="inner_modes",
    )(place, scale, state, state, state, sponge, inv_dr, target, table, edge, resident(near), resident(far))


IN_SLOTS = 3
OUT_SLOTS = 2


def update_kernel(
    place_ref, scale_ref, inv_dr_ref, target_ref, near_ref, halo_ref, behind_ref, state_ref, level_ref,
    out_ref, ahead_ref, rows_ref, fields_ref, levels_ref, result_ref, axial_even_ref, axial_odd_ref, swirl_even_ref,
    swirl_odd_ref, base_ref, field_sem, level_sem, result_sem, *, cells, chunk, unroll,
):
    axial_refs = (axial_even_ref, axial_odd_ref)
    swirl_refs = (swirl_even_ref, swirl_odd_ref)
    planes, columns, cycles = level_ref.shape
    tiles = cycles // LANES - 1
    odd = place_ref[0]
    rest = pl.ds(LANES, cycles - LANES)
    lane = lax.broadcasted_iota(jnp.int32, (chunk, LANES), 1)

    def fetch(plane):
        slot = lax.rem(plane, IN_SLOTS)
        return (
            pltpu.make_async_copy(state_ref.at[:, plane, :, rest], fields_ref.at[slot], field_sem.at[slot]),
            pltpu.make_async_copy(level_ref.at[plane, :, rest], levels_ref.at[slot], level_sem.at[slot]),
        )

    def store(plane):
        slot = lax.rem(plane, OUT_SLOTS)
        return pltpu.make_async_copy(result_ref.at[slot], out_ref.at[:, plane, :, rest], result_sem.at[slot])

    for plane in range(IN_SLOTS):
        for copy in fetch(plane):
            copy.start()

    fill_rows(rows_ref, inv_dr_ref[:, LANES:], LANES, cycles, cells)

    def wide(k, tile):
        row = rows_ref[k, :, tile * LANES : (tile + 1) * LANES]
        return jnp.broadcast_to(row[None], (chunk // 8, 8, LANES)).reshape(chunk, LANES)

    def outside(c, use):
        rows = pl.ds(pl.multiple_of(c * chunk, chunk), chunk)
        return [[jnp.where(use, near_ref[f, rows, (k + 1) * LANES : (k + 2) * LANES], 0.0) for f in range(5)] for k in range(tiles)]

    def before(c, _):
        axial = outside(c, odd == 1)
        for k in range(tiles):
            for f in range(5):
                axial_odd_ref[f, k, pl.ds(pl.multiple_of(c * chunk, chunk), chunk)] = axial[k][f]
        return 0

    lax.fori_loop(0, columns // chunk, before, 0)

    def finish(plane, parity, start, k, axial):
        rows = pl.ds(start, chunk)
        factor = (0.5 * time_step) * scale_ref[jnp.maximum(plane - 1, 0)]
        axial_ref, swirl_ref = axial_refs[parity], swirl_refs[1 - parity]
        slot = lax.rem(plane + OUT_SLOTS - 1, OUT_SLOTS)
        for f in range(5):
            value = base_ref[f, k, rows] - factor * (axial[f] - axial_ref[f, k, rows])
            value = value + (
                swirl_ref[f, k, pl.ds(start + 7, chunk)] - swirl_ref[f, k, pl.ds(start + 9, chunk)]
            )
            result_ref[slot, f, rows, k * LANES : (k + 1) * LANES] = value

    def one_chunk(plane, parity, c):
        start = pl.multiple_of(c * chunk, chunk)
        rows = pl.ds(start, chunk)
        slot = lax.rem(plane, IN_SLOTS)

        def open_tile(k):
            q = [fields_ref[slot, f, rows, k * LANES : (k + 1) * LANES] for f in range(5)]
            axial, radial, swirl = all_fluxes(q)
            ahead = [pltpu.roll(flux, LANES - 1, 1) for flux in radial]
            behind = [pltpu.roll(flux, 1, 1) for flux in radial]
            return q, axial, swirl, ahead, behind

        def close_tile(k, last, this, following):
            q, axial, swirl, ahead, behind = this
            if following is not None:
                ahead = [jnp.where(lane == LANES - 1, following[3][f], ahead[f]) for f in range(5)]
            if last is not None:
                first = last[4]
            else:
                first = [behind_ref[f, plane, rows] for f in range(5)]
                for f in range(5):
                    ahead_ref[f, plane, rows] = this[3][f]
            behind = [jnp.where(lane == 0, first[f], behind[f]) for f in range(5)]
            sponge = levels_ref[slot, rows, k * LANES : (k + 1) * LANES].astype(jnp.float32) * (
                time_step * sponge_rate
            )
            target = [
                jnp.broadcast_to(target_ref[f : f + 1, (k + 1) * LANES : (k + 2) * LANES], (chunk, LANES))
                for f in range(5)
            ]
            around = wide(2, k)
            scaled = [around * flux for flux in swirl]
            base = base_update(q, sponge, target, ahead, behind, wide(0, k), wide(1, k), scaled, cells)
            finish(plane, parity, start, k, axial)
            for f in range(5):
                base_ref[f, k, rows] = base[f]
                axial_refs[parity][f, k, rows] = axial[f]
                swirl_refs[parity][f, k, pl.ds(start + 8, chunk)] = scaled[f]

        opened = [open_tile(0)]
        for k in range(tiles):
            if k + 1 < tiles:
                opened.append(open_tile(k + 1))
            close_tile(
                k, opened[k - 1] if k else None, opened[k], opened[k + 1] if k + 1 < tiles else None
            )

    def one_plane(plane, parity):
        for copy in fetch(plane):
            copy.wait()
        for f in range(5):
            for side, row in ((0, 7), (1, columns + 8)):
                edge = halo_ref[side, f, pl.ds(plane, 1), :]
                for k in range(tiles):
                    around = rows_ref[2, 0:1, k * LANES : (k + 1) * LANES]
                    swirl_refs[parity][f, k, row : row + 1] = around * edge[:, (k + 1) * LANES : (k + 2) * LANES]
        pl.when(plane > OUT_SLOTS)(lambda: store(plane - 1 - OUT_SLOTS).wait())

        def step(c, _):
            one_chunk(plane, parity, c)
            return 0

        lax.fori_loop(0, columns // chunk, step, 0, unroll=unroll)
        pl.when(plane > 0)(lambda: store(plane - 1).start())

        @pl.when(plane + IN_SLOTS < planes)
        def _():
            for copy in fetch(plane + IN_SLOTS):
                copy.start()

    def two_planes(pair, _):
        for parity in range(2):
            one_plane(2 * pair + parity, parity)
        return 0

    lax.fori_loop(0, planes // 2, two_planes, 0)
    store(planes - 1 - OUT_SLOTS).wait()

    def last(c, _):
        start = pl.multiple_of(c * chunk, chunk)
        axial = outside(c, odd == 0)
        for k in range(tiles):
            finish(planes, 0, start, k, axial[k])
        return 0

    lax.fori_loop(0, columns // chunk, last, 0)
    store(planes - 1).start()
    for plane in range(planes - OUT_SLOTS, planes):
        store(plane).wait()


def bulk_update(place, scale, state, sponge, inv_dr, target, near, halo, behind, cells, chunk=8, unroll=16):
    _, planes, columns, cycles = state.shape
    tiles = cycles // LANES - 1
    width = cycles - LANES
    return pl.pallas_call(
        functools.partial(update_kernel, cells=cells, chunk=chunk, unroll=unroll),
        in_specs=[SMEM_SPEC, SMEM_SPEC, VMEM_SPEC, VMEM_SPEC, VMEM_SPEC, VMEM_SPEC, VMEM_SPEC, HBM_SPEC, HBM_SPEC],
        out_specs=[HBM_SPEC, VMEM_SPEC],
        scratch_shapes=[
            pltpu.VMEM((3, 8, width), jnp.float32),
            pltpu.VMEM((IN_SLOTS, 5, columns, width), jnp.float32),
            pltpu.VMEM((IN_SLOTS, columns, width), jnp.int32),
            pltpu.VMEM((OUT_SLOTS, 5, columns, width), jnp.float32),
            pltpu.VMEM((5, tiles, columns, LANES), jnp.float32),
            pltpu.VMEM((5, tiles, columns, LANES), jnp.float32),
            pltpu.VMEM((5, tiles, columns + 16, LANES), jnp.float32),
            pltpu.VMEM((5, tiles, columns + 16, LANES), jnp.float32),
            pltpu.VMEM((5, tiles, columns, LANES), jnp.float32),
            pltpu.SemaphoreType.DMA((IN_SLOTS,)),
            pltpu.SemaphoreType.DMA((IN_SLOTS,)),
            pltpu.SemaphoreType.DMA((OUT_SLOTS,)),
        ],
        out_shape=[
            jax.ShapeDtypeStruct(state.shape, jnp.float32),
            pltpu.VMEM((5, planes, columns, LANES), jnp.float32),
        ],
        compiler_params=pltpu.CompilerParams(vmem_limit_bytes=20 * MIB),
        name="bulk_update",
    )(place, scale, inv_dr, target, resident(near), resident(halo), resident(behind), state, sponge)


def filter_kernel(
    place_ref, cutoff_ref, table_ref, inv_dr_ref, tile_ref, ahead_ref, halo_ref, *refs, cells, cycles
):
    *sums, state_ref, out_ref, split_ref = refs
    step = pl.program_id(0)
    steps = pl.num_programs(0)
    half = table_ref.shape[2] // 4
    count = half // 2
    columns = out_ref.shape[2]
    mode = lax.broadcasted_iota(jnp.int32, (half, LANES), 0)
    mode = jnp.where(mode >= count, mode - count, mode) + 1
    cut = jnp.concatenate([cutoff_ref[...]] * PACK, axis=1)
    weight = jnp.where(mode <= cut, 2.0 / cells, 0.0)
    lane = lax.broadcasted_iota(jnp.int32, (columns, LANES), 1)
    spacing = 4.0 / cycles
    edge = 1.0 + spacing * (LANES - 1)
    up = (0.5 * time_step) * inv_dr_ref[...] * ((edge + spacing) / edge)
    up = jnp.where(lane == LANES - 1, up, 0.0)
    cycle = lax.broadcasted_iota(jnp.int32, (1, LANES), 1)
    around = (time_step * cells / (4.0 * math.pi)) / (1.0 + spacing * cycle.astype(jnp.float32))
    around = jnp.where(cycle < CYCLE, 0.0, around)
    for f in range(5):
        group = step * 5 + f
        rows = pl.ds(pl.multiple_of(group * half, half), half)
        coefficient = sums[0][rows, :]
        mean = sums[0][pl.ds(steps * 5 * half + group, 1), :]
        for other in sums[1:]:
            coefficient = coefficient + other[rows, :]
            mean = mean + other[pl.ds(steps * 5 * half + group, 1), :]
        coefficient = coefficient * weight
        high = coefficient.astype(jnp.bfloat16)
        low = (coefficient - high.astype(jnp.float32)).astype(jnp.bfloat16)
        for k in range(2):
            split_ref[f, 2 * k * half : (2 * k + 1) * half] = high
            split_ref[f, (2 * k + 1) * half : (2 * k + 2) * half] = low
        values = jnp.dot(table_ref[0], split_ref[f], preferred_element_type=jnp.float32) + mean * (1.0 / cells)
        for i in range(PACK):
            turned = values if i == 0 else pltpu.roll(values, LANES - i * CYCLE, 1)
            plane = step * PACK + i
            out_ref[f, i] = jnp.where(lane < CYCLE, turned, tile_ref[f, plane] - up * ahead_ref[f, plane])
            low = halo_ref[0, f, pl.ds(plane, 1), :][:, :LANES]
            high = halo_ref[1, f, pl.ds(plane, 1), :][:, :LANES]
            out_ref[f, i, 0:1] = out_ref[f, i, 0:1] + around * low
            out_ref[f, i, columns - 1 : columns] = out_ref[f, i, columns - 1 : columns] - around * high


def put_filtered(place, cutoff, table, inv_dr, tile, ahead, halo, sums, updated, cells):
    _, planes, columns, cycles = updated.shape
    return pl.pallas_call(
        functools.partial(filter_kernel, cells=cells, cycles=cycles),
        grid_spec=pltpu.PrefetchScalarGridSpec(
            num_scalar_prefetch=1,
            grid=(planes // PACK,),
            in_specs=[
                pl.BlockSpec(cutoff.shape, lambda g, place: (0, 0)),
                pl.BlockSpec((1,) + table.shape[1:], lambda g, place: (place[1], 0, 0)),
                pl.BlockSpec((1, LANES), lambda g, place: (0, 0)),
                VMEM_SPEC,
                VMEM_SPEC,
                VMEM_SPEC,
            ]
            + [VMEM_SPEC] * len(sums)
            + [HBM_SPEC],
            out_specs=pl.BlockSpec((5, PACK, columns, LANES), lambda g, place: (0, g, 0, 0)),
            scratch_shapes=[pltpu.VMEM((5, table.shape[2], LANES), jnp.bfloat16)],
        ),
        out_shape=jax.ShapeDtypeStruct(updated.shape, jnp.float32),
        input_output_aliases={7 + len(sums): 0},
        compiler_params=params(1, 12),
        name="put_filtered",
    )(place, cutoff, table, inv_dr, resident(tile), resident(ahead), resident(halo),
      *(resident(part) for part in sums), updated)


def finish_kernel(place_ref, scale_ref, flux_ref, state_ref, out_ref):
    odd = place_ref[0]
    planes = scale_ref.shape[0]
    rows = out_ref.shape[2]
    factor = (0.5 * time_step) * scale_ref[odd * (planes - 1)]
    factor = jnp.where(odd == 1, -factor, factor)
    lane = lax.broadcasted_iota(jnp.int32, out_ref.shape[2:], 1)
    start = pl.multiple_of(pl.program_id(0) * rows, 8)
    for f in range(5):
        out_ref[f, 0] = state_ref[f, 0] + jnp.where(lane < CYCLE, 0.0, factor * flux_ref[f, pl.ds(start, rows)])


def finish_plane(place, scale, flux, updated):
    _, planes, columns, cycles = updated.shape
    steps = 2
    block = pl.BlockSpec((5, 1, columns // steps, cycles), lambda b, place: (0, place[0] * (planes - 1), b, 0))
    return pl.pallas_call(
        finish_kernel,
        grid_spec=pltpu.PrefetchScalarGridSpec(
            num_scalar_prefetch=1,
            grid=(steps,),
            in_specs=[SMEM_SPEC, VMEM_SPEC, block],
            out_specs=block,
        ),
        out_shape=jax.ShapeDtypeStruct(updated.shape, jnp.float32),
        input_output_aliases={3: 0},
        compiler_params=params(1, 12),
        name="finish_plane",
    )(place, scale, resident(flux), updated)


def mode_tables(cells, sectors):
    columns = cells // sectors
    mode = np.arange(1, cells // 8 + 1)

    def waves(cell):
        angle = 2.0 * np.pi / cells * ((mode[:, None] * cell[None, :]) % cells)
        return np.concatenate([np.cos(angle), np.sin(angle)])

    forward, inverse, edge = [], [], []
    for sector in range(sectors):
        wave = waves(sector * columns + np.arange(columns))
        high = wave.astype(ml_dtypes.bfloat16)
        low = (wave - high.astype(np.float64)).astype(ml_dtypes.bfloat16)
        forward.append(np.block([[high, high], [low, low]]))
        inverse.append(np.concatenate([high.T, high.T, low.T, low.T], axis=1))
        ends = waves(np.array([sector * columns - 1, (sector + 1) * columns]) % cells)
        edge.append(np.broadcast_to(ends.T[:, :, None], (2, ends.shape[0], LANES)))
    return np.stack(forward), np.stack(inverse), np.stack(edge).astype(np.float32)


def body(forward, inverse, edge, cells, state, sponge_level, inv_dx, inv_dr, target, cutoff):
    sectors = lax.axis_size("az")
    rows = lax.axis_size("gx")
    place = jnp.stack([lax.rem(lax.axis_index("gx"), 2), lax.axis_index("az")]).astype(jnp.int32)
    cycles = state.shape[3]
    inv_dr = inv_dr.reshape(1, cycles)
    cutoff = cutoff.reshape(1, CYCLE)

    near_pairs = [(i ^ 1, i) for i in range(rows) if i ^ 1 < rows]
    far_pairs = [(i, i + 1) for i in range(1, rows - 1, 2)] + [(i + 1, i) for i in range(1, rows - 1, 2)]
    shifted = lambda part, by: lax.ppermute(part, "az", [(i, (i + by) % sectors) for i in range(sectors)])

    far_flux, far_packed = outer_plane(place, state)
    far_packed = lax.ppermute(far_packed, "gx", far_pairs)
    far_flux = lax.ppermute(far_flux, "gx", far_pairs)
    near_flux, edges = inner_plane(place, state)
    near_flux = lax.ppermute(near_flux, "gx", near_pairs)
    if sectors == 2:
        halo = shifted(edges, 1)
    else:
        halo = jnp.stack([shifted(edges[0], 1), shifted(edges[1], sectors - 1)])
    sums, tile, behind = inner_modes(
        place, inv_dx, state, sponge_level, inv_dr, target, forward, edge, near_flux, far_packed, cells
    )
    others = [shifted(sums, by) for by in range(1, sectors)]
    updated, ahead = bulk_update(
        place, inv_dx, state, sponge_level, inv_dr, target, near_flux, halo, behind, cells
    )
    updated = put_filtered(place, cutoff, inverse, inv_dr, tile, ahead, halo, [sums, *others], updated, cells)
    return finish_plane(place, inv_dx, far_flux, updated)


def solution(mesh):
    def whole(state, sponge_level, inv_dx, inv_dr, target, cutoff):
        cells = state.shape[2]
        tables = mode_tables(cells, mesh.shape["az"])
        mapped = jax.shard_map(
            functools.partial(body, *(jnp.asarray(table) for table in tables), cells),
            mesh=mesh,
            in_specs=(P(None, "gx", "az", None), P("gx", "az", None), P("gx"), P(), P(), P()),
            out_specs=P(None, "gx", "az", None),
            check_vma=False,
        )
        return mapped(state, sponge_level, inv_dx, inv_dr, target, cutoff)

    return whole
```

```python
import functools
import math

import jax
import jax.numpy as jnp
import ml_dtypes
import numpy as np
from jax import lax
from jax.experimental import pallas as pl
from jax.experimental.pallas import tpu as pltpu
from jax.sharding import PartitionSpec as P

CYCLE = 32
LANES = 128
PACK = LANES // CYCLE

gas_factor = 0.4
time_step = 0.02
sponge_rate = 4.0

MIB = 1024 * 1024


def params(steps, limit):
    return pltpu.CompilerParams(
        dimension_semantics=("arbitrary",) * steps, vmem_limit_bytes=limit * MIB
    )


def resident(x):
    return pltpu.with_memory_space_constraint(x, pltpu.VMEM)


VMEM_SPEC = pl.BlockSpec(memory_space=pltpu.VMEM)
SMEM_SPEC = pl.BlockSpec(memory_space=pltpu.SMEM)
HBM_SPEC = pl.BlockSpec(memory_space=pl.ANY)


def products(q):
    density, m, n, s, energy = q
    inverse = pltpu.reciprocal(density, approx=True)
    u, v, w = m * inverse, n * inverse, s * inverse
    mu, nv, sw = m * u, n * v, s * w
    pressure = gas_factor * energy - (0.5 * gas_factor) * (mu + nv + sw)
    return u, v, w, mu, nv, sw, pressure, energy + pressure


def axial_flux(q):
    u, _, _, mu, _, _, pressure, enthalpy = products(q)
    return (q[1], mu + pressure, q[2] * u, q[3] * u, enthalpy * u)


def swirl_flux(q):
    _, _, w, _, _, sw, pressure, enthalpy = products(q)
    return (q[3], q[1] * w, q[2] * w, sw + pressure, enthalpy * w)


def all_fluxes(q):
    u, v, w, mu, nv, sw, pressure, enthalpy = products(q)
    mv, mw, nw = q[1] * v, q[1] * w, q[2] * w
    axial = (q[1], mu + pressure, mv, mw, enthalpy * u)
    radial = (q[2], mv, nv + pressure, nw, enthalpy * v)
    swirl = (q[3], mw, nw, sw + pressure, enthalpy * w)
    return axial, radial, swirl


def fill_rows(rows_ref, inv_dr, start, cycles, cells):
    width = rows_ref.shape[-1]
    cycle = lax.broadcasted_iota(jnp.int32, (8, width), 1) + start
    spacing = 4.0 / cycles
    radius = 1.0 + spacing * cycle.astype(jnp.float32)
    inverse = 1.0 / radius
    half = (0.5 * time_step) * jnp.broadcast_to(inv_dr, (8, width)) * inverse
    rows_ref[0] = jnp.where(cycle == start + width - 1, 0.0, half * (radius + spacing))
    rows_ref[1] = jnp.where(cycle == 0, 0.0, half * (radius - spacing))
    rows_ref[2] = (time_step * cells / (4.0 * math.pi)) * inverse


def base_update(q, sponge, target, ahead, behind, up, down, scaled, cells):
    source = 4.0 * math.pi / cells
    result = []
    for f in range(5):
        value = q[f] - sponge * (q[f] - target[f]) - (up * ahead[f] - down * behind[f])
        if f == 2:
            value = value + source * scaled[3]
        if f == 3:
            value = value - source * scaled[2]
        result.append(value)
    return result


def edge_kernel(place_ref, state_ref, first_ref, last_ref, near_ref, edge_ref, packed_ref, flux_ref):
    step = pl.program_id(0)
    rows = packed_ref.shape[1]
    blocks = state_ref.shape[2] // rows
    low = swirl_flux([last_ref[f, :, 7, :] for f in range(5)])
    high = swirl_flux([first_ref[f, :, 0, :] for f in range(5)])
    planes = pl.ds(pl.multiple_of(step * 8, 8), 8)
    flux = axial_flux([state_ref[f, 0] for f in range(5)])
    lane = lax.broadcasted_iota(jnp.int32, packed_ref.shape[1:], 1)
    for f in range(5):
        edge_ref[0, f, planes] = low[f]
        edge_ref[1, f, planes] = high[f]
        for i in range(blocks):
            block = step * blocks + i
            turned = pltpu.roll(flux[f][i * rows : (i + 1) * rows], block * CYCLE, 1)
            packed_ref[f] = jnp.where(lane // CYCLE == block, turned, packed_ref[f])
    flux = axial_flux([near_ref[f, 0] for f in range(5)])
    count = near_ref.shape[2]
    for f in range(5):
        flux_ref[f, pl.ds(pl.multiple_of(step * count, 8), count)] = flux[f]


def edge_cells(place, state):
    _, planes, columns, cycles = state.shape
    steps = planes // 8
    return pl.pallas_call(
        edge_kernel,
        grid_spec=pltpu.PrefetchScalarGridSpec(
            num_scalar_prefetch=1,
            grid=(steps,),
            in_specs=[
                pl.BlockSpec((5, 1, columns // steps, LANES), lambda b, place: (0, place[0] * (planes - 1), b, 0)),
                pl.BlockSpec((5, 8, 8, cycles), lambda b, place: (0, b, 0, 0)),
                pl.BlockSpec((5, 8, 8, cycles), lambda b, place: (0, b, columns // 8 - 1, 0)),
                pl.BlockSpec(
                    (5, 1, columns // steps, cycles), lambda b, place: (0, (1 - place[0]) * (planes - 1), b, 0)
                ),
            ],
            out_specs=[VMEM_SPEC, VMEM_SPEC, VMEM_SPEC],
        ),
        out_shape=[
            pltpu.VMEM((2, 5, planes, cycles), jnp.float32),
            pltpu.VMEM((5, columns // PACK, LANES), jnp.float32),
            pltpu.VMEM((5, columns, cycles), jnp.float32),
        ],
        compiler_params=params(1, 8),
        name="edge_cells",
    )(place, state, state, state, state)


def outer_kernel(place_ref, state_ref, *refs):
    flux_ref = refs[-1]
    count = state_ref.shape[2]
    rows = pl.ds(pl.multiple_of(pl.program_id(0) * count, 8), count)
    flux = axial_flux([state_ref[f, 0] for f in range(5)])
    for f in range(5):
        flux_ref[f, rows] = flux[f]


def outer_plane(place, state, after):
    _, planes, columns, cycles = state.shape
    steps = 2
    return pl.pallas_call(
        outer_kernel,
        grid_spec=pltpu.PrefetchScalarGridSpec(
            num_scalar_prefetch=1,
            grid=(steps,),
            in_specs=[
                pl.BlockSpec((5, 1, columns // steps, cycles), lambda b, place: (0, place[0] * (planes - 1), b, 0)),
            ]
            + [VMEM_SPEC] * len(after),
            out_specs=VMEM_SPEC,
        ),
        out_shape=pltpu.VMEM((5, columns, cycles), jnp.float32),
        compiler_params=params(1, 8),
        name="outer_plane",
    )(place, state, *(resident(part) for part in after))


def modes_kernel(
    place_ref, scale_ref, state_ref, before_ref, after_ref, level_ref, inv_dr_ref, target_ref, table_ref, edge_ref,
    *refs, cycles, cells, chunk, pick, steps, outside,
):
    if outside:
        near_ref, far_ref = refs[:2]
    sums_ref, tile_ref, behind_ref, rows_ref, axial_ref, swirl_ref, base_ref, split_ref = refs[-8:]
    step = pick(pl.program_id(0))
    columns = state_ref.shape[2]
    odd = place_ref[0]

    @pl.when(pl.program_id(0) == 0)
    def _():
        fill_rows(rows_ref, inv_dr_ref[...], 0, cycles, cells)
        for f in range(5):
            for i in range(PACK):
                swirl_ref[i, f, 0:8] = jnp.zeros((8, LANES), jnp.float32)
                swirl_ref[i, f, columns + 8 : columns + 16] = jnp.zeros((8, LANES), jnp.float32)

    def load(ref, plane, start):
        return [ref[f, plane, pl.ds(start, chunk), :] for f in range(5)]

    def halo(slot, use_near):
        far_rows = far_ref.shape[1]
        for f in range(5):
            for b in range(PACK):
                away = far_ref[f]
                away = away if b == 0 else pltpu.roll(away, LANES - b * CYCLE, 1)
                near = near_ref[f, b * far_rows : (b + 1) * far_rows, :LANES]
                axial_ref[slot, f, b * far_rows : (b + 1) * far_rows] = jnp.where(
                    use_near, near, jnp.where(lane[:far_rows] < CYCLE, away, 0.0)
                )

    def neighbour(slot, ref):
        def one(c, _):
            start = pl.multiple_of(c * chunk, chunk)
            flux = axial_flux(load(ref, 0, start))
            for f in range(5):
                axial_ref[slot, f, pl.ds(start, chunk)] = flux[f]
            return 0

        lax.fori_loop(0, columns // chunk, one, 0, unroll=True)

    lane = lax.broadcasted_iota(jnp.int32, (chunk, LANES), 1)
    if outside:
        pl.when(step == 0)(lambda: halo(0, odd == 1))
        pl.when(step > 0)(lambda: neighbour(0, before_ref))
        pl.when(step == steps - 1)(lambda: halo(PACK + 1, odd == 0))
        pl.when(step < steps - 1)(lambda: neighbour(PACK + 1, after_ref))
    else:
        neighbour(0, before_ref)
        neighbour(PACK + 1, after_ref)

    def wide(row):
        return jnp.broadcast_to(row[None], (chunk // 8, 8, LANES)).reshape(chunk, LANES)

    def first(c, _):
        start = pl.multiple_of(c * chunk, chunk)
        up, down, around = [wide(rows_ref[k]) for k in range(3)]
        target = [jnp.broadcast_to(target_ref[f : f + 1], (chunk, LANES)) for f in range(5)]
        for i in range(PACK):
            q = load(state_ref, i, start)
            axial, radial, swirl = all_fluxes(q)
            sponge = level_ref[i, pl.ds(start, chunk), :].astype(jnp.float32) * (time_step * sponge_rate)
            scaled = [around * flux for flux in swirl]
            ahead = [pltpu.roll(flux, LANES - 1, 1) for flux in radial]
            behind = [pltpu.roll(flux, 1, 1) for flux in radial]
            base = base_update(q, sponge, target, ahead, behind, up, down, scaled, cells)
            plane = step * PACK + i
            for f in range(5):
                behind_ref[f, plane, pl.ds(start, chunk)] = behind[f]
                axial_ref[i + 1, f, pl.ds(start, chunk)] = axial[f]
                swirl_ref[i, f, pl.ds(start + 8, chunk)] = scaled[f]
                base_ref[i, f, pl.ds(start, chunk)] = base[f]
        return 0

    lax.fori_loop(0, columns // chunk, first, 0, unroll=True)

    def packed(parts, rows):
        result = parts[0]
        for i in range(1, PACK):
            result = jnp.where(lane[:rows] // CYCLE == i, pltpu.roll(parts[i], i * CYCLE, 1), result)
        return result

    factor = [(0.5 * time_step) * scale_ref[step * PACK + i] for i in range(PACK)]
    for f in range(5):
        total = jnp.zeros((8, LANES), jnp.float32)
        for c in range(columns // chunk):
            start = c * chunk
            parts = []
            for i in range(PACK):
                value = base_ref[i, f, start : start + chunk]
                value = value - factor[i] * (
                    axial_ref[i + 2, f, start : start + chunk] - axial_ref[i, f, start : start + chunk]
                )
                inside = value + (
                    swirl_ref[i, f, start + 7 : start + 7 + chunk] - swirl_ref[i, f, start + 9 : start + 9 + chunk]
                )
                tile_ref[f, step * PACK + i, start : start + chunk] = inside
                parts.append(inside)
            value = packed(parts, chunk)
            high = value.astype(jnp.bfloat16)
            split_ref[f, start : start + chunk] = high
            split_ref[f, columns + start : columns + start + chunk] = (value - high.astype(jnp.float32)).astype(
                jnp.bfloat16
            )
            total = total + value.reshape(chunk // 8, 8, LANES).sum(axis=0)
        sums = jnp.dot(table_ref[0], split_ref[f], preferred_element_type=jnp.float32)
        half = sums.shape[0] // 2
        start_row = packed([swirl_ref[i, f, 8:16] for i in range(PACK)], 8)[0:1]
        end_row = packed([swirl_ref[i, f, columns : columns + 8] for i in range(PACK)], 8)[7:8]
        group = step * 5 + f
        sums_ref[pl.ds(pl.multiple_of(group * half, half), half), :] = (
            sums[:half] + sums[half:] + (edge_ref[0, 1] * end_row - edge_ref[0, 0] * start_row)
        )
        mean = total.sum(axis=0, keepdims=True) + (end_row - start_row)
        sums_ref[pl.ds(steps * 5 * half + group, 1), :] = mean


def mode_rows(planes, half):
    groups = 5 * planes // PACK
    return groups * half + -(-groups // 8) * 8


def inner_modes(place, scale, state, sponge, inv_dr, target, table, edge, cells, done=(), near=None, far=None):
    _, planes, columns, cycles = state.shape
    half = table.shape[1] // 2
    chunk = min(32, columns)
    steps = planes // PACK
    outside = bool(done)
    pick = (lambda g: g * (steps - 1)) if outside else (lambda g: g + 1)
    whole = lambda *shape: pl.BlockSpec(shape, lambda g, place: (0,) * len(shape))
    tile = pltpu.VMEM((5, planes, columns, LANES), jnp.float32)
    extra = [resident(part) for part in ((near, far) + tuple(done) if outside else ())]
    before = lambda g, place: (0, jnp.maximum(pick(g) * PACK - 1, 0), 0, 0)
    behind = lambda g, place: (0, jnp.minimum(pick(g) * PACK + PACK, planes - 1), 0, 0)
    return pl.pallas_call(
        functools.partial(
            modes_kernel, cycles=cycles, cells=cells, chunk=chunk, pick=pick, steps=steps, outside=outside
        ),
        grid_spec=pltpu.PrefetchScalarGridSpec(
            num_scalar_prefetch=1,
            grid=(2 if outside else steps - 2,),
            in_specs=[
                SMEM_SPEC,
                pl.BlockSpec((5, PACK, columns, LANES), lambda g, place: (0, pick(g), 0, 0)),
                pl.BlockSpec((5, 1, columns, LANES), before),
                pl.BlockSpec((5, 1, columns, LANES), behind),
                pl.BlockSpec((PACK, columns, LANES), lambda g, place: (pick(g), 0, 0)),
                whole(1, LANES),
                whole(5, LANES),
                pl.BlockSpec((1,) + table.shape[1:], lambda g, place: (place[1], 0, 0)),
                pl.BlockSpec((1,) + edge.shape[1:], lambda g, place: (place[1], 0, 0, 0)),
            ]
            + [VMEM_SPEC] * len(extra),
            out_specs=[VMEM_SPEC, VMEM_SPEC, VMEM_SPEC],
            scratch_shapes=[
                pltpu.VMEM((3, 8, LANES), jnp.float32),
                pltpu.VMEM((PACK + 2, 5, columns, LANES), jnp.float32),
                pltpu.VMEM((PACK, 5, columns + 16, LANES), jnp.float32),
                pltpu.VMEM((PACK, 5, columns, LANES), jnp.float32),
                pltpu.VMEM((5, 2 * columns, LANES), jnp.bfloat16),
            ],
        ),
        out_shape=[pltpu.VMEM((mode_rows(planes, half), LANES), jnp.float32), tile, tile],
        input_output_aliases={12 + k: k for k in range(3)} if outside else {},
        compiler_params=params(1, 20),
        name="end_modes" if outside else "middle_modes",
    )(place, scale, state, state, state, sponge, inv_dr, target, table, edge, *extra)


IN_SLOTS = 3
OUT_SLOTS = 2


def update_kernel(
    place_ref, scale_ref, inv_dr_ref, target_ref, near_ref, halo_ref, behind_ref, state_ref, level_ref,
    out_ref, ahead_ref, kept_ref, rows_ref, fields_ref, levels_ref, result_ref, axial_even_ref, axial_odd_ref, swirl_even_ref,
    swirl_odd_ref, base_ref, field_sem, level_sem, result_sem, *, cells, chunk, unroll,
):
    axial_refs = (axial_even_ref, axial_odd_ref)
    swirl_refs = (swirl_even_ref, swirl_odd_ref)
    planes, columns, cycles = level_ref.shape
    tiles = cycles // LANES - 1
    odd = place_ref[0]
    rest = pl.ds(LANES, cycles - LANES)
    lane = lax.broadcasted_iota(jnp.int32, (chunk, LANES), 1)

    def fetch(plane):
        slot = lax.rem(plane, IN_SLOTS)
        return (
            pltpu.make_async_copy(state_ref.at[:, plane, :, rest], fields_ref.at[slot], field_sem.at[slot]),
            pltpu.make_async_copy(level_ref.at[plane, :, rest], levels_ref.at[slot], level_sem.at[slot]),
        )

    def store(plane):
        slot = lax.rem(plane, OUT_SLOTS)
        return pltpu.make_async_copy(result_ref.at[slot], out_ref.at[:, plane, :, rest], result_sem.at[slot])

    def keep(plane):
        slot = lax.rem(plane, OUT_SLOTS)
        return pltpu.make_async_copy(result_ref.at[slot], kept_ref, result_sem.at[slot])

    for plane in range(IN_SLOTS):
        for copy in fetch(plane):
            copy.start()

    fill_rows(rows_ref, inv_dr_ref[:, LANES:], LANES, cycles, cells)

    def wide(k, tile):
        row = rows_ref[k, :, tile * LANES : (tile + 1) * LANES]
        return jnp.broadcast_to(row[None], (chunk // 8, 8, LANES)).reshape(chunk, LANES)

    def outside(c, use):
        rows = pl.ds(pl.multiple_of(c * chunk, chunk), chunk)
        return [[jnp.where(use, near_ref[f, rows, (k + 1) * LANES : (k + 2) * LANES], 0.0) for f in range(5)] for k in range(tiles)]

    def before(c, _):
        axial = outside(c, odd == 1)
        for k in range(tiles):
            for f in range(5):
                axial_odd_ref[f, k, pl.ds(pl.multiple_of(c * chunk, chunk), chunk)] = axial[k][f]
        return 0

    lax.fori_loop(0, columns // chunk, before, 0)

    def finish(plane, parity, start, k, axial):
        rows = pl.ds(start, chunk)
        factor = (0.5 * time_step) * scale_ref[jnp.maximum(plane - 1, 0)]
        axial_ref, swirl_ref = axial_refs[parity], swirl_refs[1 - parity]
        slot = lax.rem(plane + OUT_SLOTS - 1, OUT_SLOTS)
        for f in range(5):
            value = base_ref[f, k, rows] - factor * (axial[f] - axial_ref[f, k, rows])
            value = value + (
                swirl_ref[f, k, pl.ds(start + 7, chunk)] - swirl_ref[f, k, pl.ds(start + 9, chunk)]
            )
            result_ref[slot, f, rows, k * LANES : (k + 1) * LANES] = value

    def one_chunk(plane, parity, c):
        start = pl.multiple_of(c * chunk, chunk)
        rows = pl.ds(start, chunk)
        slot = lax.rem(plane, IN_SLOTS)

        def open_tile(k):
            q = [fields_ref[slot, f, rows, k * LANES : (k + 1) * LANES] for f in range(5)]
            axial, radial, swirl = all_fluxes(q)
            ahead = [pltpu.roll(flux, LANES - 1, 1) for flux in radial]
            behind = [pltpu.roll(flux, 1, 1) for flux in radial]
            return q, axial, swirl, ahead, behind

        def close_tile(k, last, this, following):
            q, axial, swirl, ahead, behind = this
            if following is not None:
                ahead = [jnp.where(lane == LANES - 1, following[3][f], ahead[f]) for f in range(5)]
            if last is not None:
                first = last[4]
            else:
                first = [behind_ref[f, plane, rows] for f in range(5)]
                for f in range(5):
                    ahead_ref[f, plane, rows] = this[3][f]
            behind = [jnp.where(lane == 0, first[f], behind[f]) for f in range(5)]
            sponge = levels_ref[slot, rows, k * LANES : (k + 1) * LANES].astype(jnp.float32) * (
                time_step * sponge_rate
            )
            target = [
                jnp.broadcast_to(target_ref[f : f + 1, (k + 1) * LANES : (k + 2) * LANES], (chunk, LANES))
                for f in range(5)
            ]
            around = wide(2, k)
            scaled = [around * flux for flux in swirl]
            base = base_update(q, sponge, target, ahead, behind, wide(0, k), wide(1, k), scaled, cells)
            finish(plane, parity, start, k, axial)
            for f in range(5):
                base_ref[f, k, rows] = base[f]
                axial_refs[parity][f, k, rows] = axial[f]
                swirl_refs[parity][f, k, pl.ds(start + 8, chunk)] = scaled[f]

        opened = [open_tile(0)]
        for k in range(tiles):
            if k + 1 < tiles:
                opened.append(open_tile(k + 1))
            close_tile(
                k, opened[k - 1] if k else None, opened[k], opened[k + 1] if k + 1 < tiles else None
            )

    def one_plane(plane, parity):
        for copy in fetch(plane):
            copy.wait()
        for f in range(5):
            for side, row in ((0, 7), (1, columns + 8)):
                edge = halo_ref[side, f, pl.ds(plane, 1), :]
                for k in range(tiles):
                    around = rows_ref[2, 0:1, k * LANES : (k + 1) * LANES]
                    swirl_refs[parity][f, k, row : row + 1] = around * edge[:, (k + 1) * LANES : (k + 2) * LANES]
        pl.when(plane > OUT_SLOTS)(lambda: store(plane - 1 - OUT_SLOTS).wait())

        def step(c, _):
            one_chunk(plane, parity, c)
            return 0

        lax.fori_loop(0, columns // chunk, step, 0, unroll=unroll)
        outer = jnp.logical_and(plane == 1, odd == 0)
        pl.when(outer)(lambda: keep(plane - 1).start())
        pl.when(jnp.logical_and(plane > 0, jnp.logical_not(outer)))(lambda: store(plane - 1).start())

        @pl.when(plane + IN_SLOTS < planes)
        def _():
            for copy in fetch(plane + IN_SLOTS):
                copy.start()

    def two_planes(pair, _):
        for parity in range(2):
            one_plane(2 * pair + parity, parity)
        return 0

    lax.fori_loop(0, planes // 2, two_planes, 0)
    store(planes - 1 - OUT_SLOTS).wait()

    def last(c, _):
        start = pl.multiple_of(c * chunk, chunk)
        axial = outside(c, odd == 0)
        for k in range(tiles):
            finish(planes, 0, start, k, axial[k])
        return 0

    lax.fori_loop(0, columns // chunk, last, 0)
    pl.when(odd == 0)(lambda: store(planes - 1).start())
    pl.when(odd == 1)(lambda: keep(planes - 1).start())
    for plane in range(planes - OUT_SLOTS, planes):
        store(plane).wait()


def bulk_update(place, scale, state, sponge, inv_dr, target, near, halo, behind, cells, chunk=8, unroll=16):
    _, planes, columns, cycles = state.shape
    tiles = cycles // LANES - 1
    width = cycles - LANES
    return pl.pallas_call(
        functools.partial(update_kernel, cells=cells, chunk=chunk, unroll=unroll),
        in_specs=[SMEM_SPEC, SMEM_SPEC, VMEM_SPEC, VMEM_SPEC, VMEM_SPEC, VMEM_SPEC, VMEM_SPEC, HBM_SPEC, HBM_SPEC],
        out_specs=[HBM_SPEC, VMEM_SPEC, VMEM_SPEC],
        scratch_shapes=[
            pltpu.VMEM((3, 8, width), jnp.float32),
            pltpu.VMEM((IN_SLOTS, 5, columns, width), jnp.float32),
            pltpu.VMEM((IN_SLOTS, columns, width), jnp.int32),
            pltpu.VMEM((OUT_SLOTS, 5, columns, width), jnp.float32),
            pltpu.VMEM((5, tiles, columns, LANES), jnp.float32),
            pltpu.VMEM((5, tiles, columns, LANES), jnp.float32),
            pltpu.VMEM((5, tiles, columns + 16, LANES), jnp.float32),
            pltpu.VMEM((5, tiles, columns + 16, LANES), jnp.float32),
            pltpu.VMEM((5, tiles, columns, LANES), jnp.float32),
            pltpu.SemaphoreType.DMA((IN_SLOTS,)),
            pltpu.SemaphoreType.DMA((IN_SLOTS,)),
            pltpu.SemaphoreType.DMA((OUT_SLOTS,)),
        ],
        out_shape=[
            jax.ShapeDtypeStruct(state.shape, jnp.float32),
            pltpu.VMEM((5, planes, columns, LANES), jnp.float32),
            pltpu.VMEM((5, columns, width), jnp.float32),
        ],
        compiler_params=pltpu.CompilerParams(vmem_limit_bytes=20 * MIB),
        name="bulk_update",
    )(place, scale, inv_dr, target, resident(near), resident(halo), resident(behind), state, sponge)


def filter_kernel(
    place_ref, cutoff_ref, table_ref, inv_dr_ref, tile_ref, ahead_ref, halo_ref, *refs, cells, cycles
):
    *sums, state_ref, out_ref, kept_ref, split_ref = refs
    step = pl.program_id(0)
    steps = pl.num_programs(0)
    half = table_ref.shape[2] // 4
    count = half // 2
    columns = out_ref.shape[2]
    mode = lax.broadcasted_iota(jnp.int32, (half, LANES), 0)
    mode = jnp.where(mode >= count, mode - count, mode) + 1
    cut = jnp.concatenate([cutoff_ref[...]] * PACK, axis=1)
    weight = jnp.where(mode <= cut, 2.0 / cells, 0.0)
    lane = lax.broadcasted_iota(jnp.int32, (columns, LANES), 1)
    spacing = 4.0 / cycles
    edge = 1.0 + spacing * (LANES - 1)
    up = (0.5 * time_step) * inv_dr_ref[...] * ((edge + spacing) / edge)
    up = jnp.where(lane == LANES - 1, up, 0.0)
    cycle = lax.broadcasted_iota(jnp.int32, (1, LANES), 1)
    around = (time_step * cells / (4.0 * math.pi)) / (1.0 + spacing * cycle.astype(jnp.float32))
    around = jnp.where(cycle < CYCLE, 0.0, around)
    for f in range(5):
        group = step * 5 + f
        rows = pl.ds(pl.multiple_of(group * half, half), half)
        coefficient = sums[0][rows, :]
        mean = sums[0][pl.ds(steps * 5 * half + group, 1), :]
        for other in sums[1:]:
            coefficient = coefficient + other[rows, :]
            mean = mean + other[pl.ds(steps * 5 * half + group, 1), :]
        coefficient = coefficient * weight
        high = coefficient.astype(jnp.bfloat16)
        low = (coefficient - high.astype(jnp.float32)).astype(jnp.bfloat16)
        for k in range(2):
            split_ref[f, 2 * k * half : (2 * k + 1) * half] = high
            split_ref[f, (2 * k + 1) * half : (2 * k + 2) * half] = low
        values = jnp.dot(table_ref[0], split_ref[f], preferred_element_type=jnp.float32) + mean * (1.0 / cells)
        for i in range(PACK):
            turned = values if i == 0 else pltpu.roll(values, LANES - i * CYCLE, 1)
            plane = step * PACK + i
            out_ref[f, i] = jnp.where(lane < CYCLE, turned, tile_ref[f, plane] - up * ahead_ref[f, plane])
            low = halo_ref[0, f, pl.ds(plane, 1), :][:, :LANES]
            high = halo_ref[1, f, pl.ds(plane, 1), :][:, :LANES]
            out_ref[f, i, 0:1] = out_ref[f, i, 0:1] + around * low
            out_ref[f, i, columns - 1 : columns] = out_ref[f, i, columns - 1 : columns] - around * high

    def keep(i):
        for f in range(5):
            kept_ref[f] = out_ref[f, i]

    odd = place_ref[0]
    pl.when(jnp.logical_and(step == 0, odd == 0))(lambda: keep(0))
    pl.when(jnp.logical_and(step == steps - 1, odd == 1))(lambda: keep(PACK - 1))


def put_filtered(place, cutoff, table, inv_dr, tile, ahead, halo, sums, updated, cells):
    _, planes, columns, cycles = updated.shape
    return pl.pallas_call(
        functools.partial(filter_kernel, cells=cells, cycles=cycles),
        grid_spec=pltpu.PrefetchScalarGridSpec(
            num_scalar_prefetch=1,
            grid=(planes // PACK,),
            in_specs=[
                pl.BlockSpec(cutoff.shape, lambda g, place: (0, 0)),
                pl.BlockSpec((1,) + table.shape[1:], lambda g, place: (place[1], 0, 0)),
                pl.BlockSpec((1, LANES), lambda g, place: (0, 0)),
                VMEM_SPEC,
                VMEM_SPEC,
                VMEM_SPEC,
            ]
            + [VMEM_SPEC] * len(sums)
            + [HBM_SPEC],
            out_specs=[pl.BlockSpec((5, PACK, columns, LANES), lambda g, place: (0, g, 0, 0)), VMEM_SPEC],
            scratch_shapes=[pltpu.VMEM((5, table.shape[2], LANES), jnp.bfloat16)],
        ),
        out_shape=[
            jax.ShapeDtypeStruct(updated.shape, jnp.float32),
            pltpu.VMEM((5, columns, LANES), jnp.float32),
        ],
        input_output_aliases={7 + len(sums): 0},
        compiler_params=params(1, 12),
        name="put_filtered",
    )(place, cutoff, table, inv_dr, resident(tile), resident(ahead), resident(halo),
      *(resident(part) for part in sums), updated)


def finish_kernel(place_ref, scale_ref, flux_ref, first_ref, rest_ref, state_ref, out_ref):
    odd = place_ref[0]
    planes = scale_ref.shape[0]
    rows = out_ref.shape[2]
    factor = (0.5 * time_step) * scale_ref[odd * (planes - 1)]
    factor = jnp.where(odd == 1, -factor, factor)
    lane = lax.broadcasted_iota(jnp.int32, (rows, LANES), 1)
    cells = pl.ds(pl.multiple_of(pl.program_id(0) * rows, 8), rows)
    for f in range(5):
        flux = factor * flux_ref[f, cells]
        out_ref[f, 0, :, :LANES] = first_ref[f, cells] + jnp.where(lane < CYCLE, 0.0, flux[:, :LANES])
        out_ref[f, 0, :, LANES:] = rest_ref[f, cells] + flux[:, LANES:]


def finish_plane(place, scale, flux, first, rest, updated):
    _, planes, columns, cycles = updated.shape
    steps = 2
    return pl.pallas_call(
        finish_kernel,
        grid_spec=pltpu.PrefetchScalarGridSpec(
            num_scalar_prefetch=1,
            grid=(steps,),
            in_specs=[SMEM_SPEC, VMEM_SPEC, VMEM_SPEC, VMEM_SPEC, HBM_SPEC],
            out_specs=pl.BlockSpec(
                (5, 1, columns // steps, cycles), lambda b, place: (0, place[0] * (planes - 1), b, 0)
            ),
        ),
        out_shape=jax.ShapeDtypeStruct(updated.shape, jnp.float32),
        input_output_aliases={5: 0},
        compiler_params=params(1, 8),
        name="finish_plane",
    )(place, scale, resident(flux), resident(first), resident(rest), updated)


def mode_tables(cells, sectors):
    columns = cells // sectors
    mode = np.arange(1, cells // 8 + 1)

    def waves(cell):
        angle = 2.0 * np.pi / cells * ((mode[:, None] * cell[None, :]) % cells)
        return np.concatenate([np.cos(angle), np.sin(angle)])

    forward, inverse, edge = [], [], []
    for sector in range(sectors):
        wave = waves(sector * columns + np.arange(columns))
        high = wave.astype(ml_dtypes.bfloat16)
        low = (wave - high.astype(np.float64)).astype(ml_dtypes.bfloat16)
        forward.append(np.block([[high, high], [low, low]]))
        inverse.append(np.concatenate([high.T, high.T, low.T, low.T], axis=1))
        ends = waves(np.array([sector * columns - 1, (sector + 1) * columns]) % cells)
        edge.append(np.broadcast_to(ends.T[:, :, None], (2, ends.shape[0], LANES)))
    return np.stack(forward), np.stack(inverse), np.stack(edge).astype(np.float32)


def body(forward, inverse, edge, cells, state, sponge_level, inv_dx, inv_dr, target, cutoff):
    sectors = lax.axis_size("az")
    rows = lax.axis_size("gx")
    place = jnp.stack([lax.rem(lax.axis_index("gx"), 2), lax.axis_index("az")]).astype(jnp.int32)
    cycles = state.shape[3]
    inv_dr = inv_dr.reshape(1, cycles)
    cutoff = cutoff.reshape(1, CYCLE)

    near_pairs = [(i ^ 1, i) for i in range(rows) if i ^ 1 < rows]
    far_pairs = [(i, i + 1) for i in range(1, rows - 1, 2)] + [(i + 1, i) for i in range(1, rows - 1, 2)]
    shifted = lambda part, by: lax.ppermute(part, "az", [(i, (i + by) % sectors) for i in range(sectors)])

    state = pltpu.with_memory_space_constraint(state, pltpu.HBM)
    edges, packed, near_flux = edge_cells(place, state)
    far_packed = lax.ppermute(packed, "gx", far_pairs)
    near_flux = lax.ppermute(near_flux, "gx", near_pairs)
    if sectors == 2:
        halo = shifted(edges, 1)
    else:
        halo = jnp.stack([shifted(edges[0], 1), shifted(edges[1], sectors - 1)])
    modes = functools.partial(
        inner_modes, place, inv_dx, state, sponge_level, inv_dr, target, forward, edge, cells
    )
    middle = modes()
    far_flux = lax.ppermute(outer_plane(place, state, [far_packed, halo, middle[0]]), "gx", far_pairs)
    sums, tile, behind = modes(done=middle, near=near_flux, far=far_packed)
    others = [shifted(sums, by) for by in range(1, sectors)]
    updated, ahead, rest = bulk_update(
        place, inv_dx, state, sponge_level, inv_dr, target, near_flux, halo, behind, cells
    )
    updated, first = put_filtered(place, cutoff, inverse, inv_dr, tile, ahead, halo, [sums, *others], updated, cells)
    return finish_plane(place, inv_dx, far_flux, first, rest, updated)


def solution(mesh):
    def whole(state, sponge_level, inv_dx, inv_dr, target, cutoff):
        cells = state.shape[2]
        tables = mode_tables(cells, mesh.shape["az"])
        mapped = jax.shard_map(
            functools.partial(body, *(jnp.asarray(table) for table in tables), cells),
            mesh=mesh,
            in_specs=(P(None, "gx", "az", None), P("gx", "az", None), P("gx"), P(), P(), P()),
            out_specs=P(None, "gx", "az", None),
            check_vma=False,
        )
        return mapped(state, sponge_level, inv_dx, inv_dr, target, cutoff)

    return whole
```

```python
import functools
import math

import jax
import jax.numpy as jnp
import ml_dtypes
import numpy as np
from jax import lax
from jax.experimental import pallas as pl
from jax.experimental.pallas import tpu as pltpu
from jax.sharding import PartitionSpec as P

CYCLE = 32
LANES = 128
PACK = LANES // CYCLE

gas_factor = 0.4
time_step = 0.02
sponge_rate = 4.0

MIB = 1024 * 1024


def params(steps, limit):
    return pltpu.CompilerParams(
        dimension_semantics=("arbitrary",) * steps, vmem_limit_bytes=limit * MIB
    )


def stored(x):
    return pltpu.with_memory_space_constraint(x, pltpu.HBM)


def resident(x):
    return pltpu.with_memory_space_constraint(x, pltpu.VMEM)


VMEM_SPEC = pl.BlockSpec(memory_space=pltpu.VMEM)
SMEM_SPEC = pl.BlockSpec(memory_space=pltpu.SMEM)
HBM_SPEC = pl.BlockSpec(memory_space=pl.ANY)


def products(q):
    density, m, n, s, energy = q
    inverse = pltpu.reciprocal(density, approx=True)
    u, v, w = m * inverse, n * inverse, s * inverse
    mu, nv, sw = m * u, n * v, s * w
    pressure = gas_factor * energy - (0.5 * gas_factor) * (mu + nv + sw)
    return u, v, w, mu, nv, sw, pressure, energy + pressure


def axial_flux(q):
    u, _, _, mu, _, _, pressure, enthalpy = products(q)
    return (q[1], mu + pressure, q[2] * u, q[3] * u, enthalpy * u)


def swirl_flux(q):
    _, _, w, _, _, sw, pressure, enthalpy = products(q)
    return (q[3], q[1] * w, q[2] * w, sw + pressure, enthalpy * w)


def all_fluxes(q):
    u, v, w, mu, nv, sw, pressure, enthalpy = products(q)
    mv, mw, nw = q[1] * v, q[1] * w, q[2] * w
    axial = (q[1], mu + pressure, mv, mw, enthalpy * u)
    radial = (q[2], mv, nv + pressure, nw, enthalpy * v)
    swirl = (q[3], mw, nw, sw + pressure, enthalpy * w)
    return axial, radial, swirl


def fill_rows(rows_ref, inv_dr, start, cycles, cells):
    width = rows_ref.shape[-1]
    cycle = lax.broadcasted_iota(jnp.int32, (8, width), 1) + start
    spacing = 4.0 / cycles
    radius = 1.0 + spacing * cycle.astype(jnp.float32)
    inverse = 1.0 / radius
    half = (0.5 * time_step) * jnp.broadcast_to(inv_dr, (8, width)) * inverse
    rows_ref[0] = jnp.where(cycle == start + width - 1, 0.0, half * (radius + spacing))
    rows_ref[1] = jnp.where(cycle == 0, 0.0, half * (radius - spacing))
    rows_ref[2] = (time_step * cells / (4.0 * math.pi)) * inverse


def base_update(q, sponge, target, ahead, behind, up, down, scaled, cells):
    source = 4.0 * math.pi / cells
    result = []
    for f in range(5):
        value = q[f] - sponge * (q[f] - target[f]) - (up * ahead[f] - down * behind[f])
        if f == 2:
            value = value + source * scaled[3]
        if f == 3:
            value = value - source * scaled[2]
        result.append(value)
    return result


def edge_kernel(place_ref, state_ref, edge_ref, far_flux_ref, near_flux_ref, row_ref, plane_ref, row_sem, plane_sem):
    _, planes, columns, cycles = state_ref.shape
    odd = place_ref[0]
    ends = [
        pltpu.make_async_copy(
            state_ref.at[:, :, pl.ds(side * (columns - 1), 1)], row_ref.at[side], row_sem.at[side]
        )
        for side in range(2)
    ]
    wholes = [
        pltpu.make_async_copy(
            state_ref.at[:, away * (planes - 1), pl.ds(part * (columns // 2), columns // 2)],
            plane_ref.at[side, :, pl.ds(part * (columns // 2), columns // 2)],
            plane_sem.at[side, part],
        )
        for side, away in enumerate((odd, 1 - odd))
        for part in range(2)
    ]
    for copy in ends + wholes:
        copy.start()
    for copy in ends:
        copy.wait()
    for side in range(2):
        flux = swirl_flux([row_ref[1 - side, f, :, 0, :] for f in range(5)])
        for f in range(5):
            edge_ref[side, f] = flux[f]
    half = columns // 2
    for side, flux_ref in enumerate((far_flux_ref, near_flux_ref)):
        for part in range(2):
            wholes[2 * side + part].wait()
            cut = slice(part * half, (part + 1) * half)
            flux = axial_flux([plane_ref[side, f, cut] for f in range(5)])
            for f in range(5):
                flux_ref[f, cut] = flux[f]


def edge_cells(place, state):
    _, planes, columns, cycles = state.shape
    flux = pltpu.VMEM((5, columns, cycles), jnp.float32)
    return pl.pallas_call(
        edge_kernel,
        in_specs=[SMEM_SPEC, HBM_SPEC],
        out_specs=[VMEM_SPEC] * 3,
        scratch_shapes=[
            pltpu.VMEM((2, 5, planes, 1, cycles), jnp.float32),
            pltpu.VMEM((2, 5, columns, cycles), jnp.float32),
            pltpu.SemaphoreType.DMA((2,)),
            pltpu.SemaphoreType.DMA((2, 2)),
        ],
        out_shape=[
            pltpu.VMEM((2, 5, planes, cycles), jnp.float32),
            flux,
            flux,
        ],
        compiler_params=pltpu.CompilerParams(vmem_limit_bytes=8 * MIB),
        name="edge_cells",
    )(place, state)


def gate_kernel(sums_ref, *refs):
    refs[-1][0:8] = sums_ref[0:8]


def gate(sums, after):
    return pl.pallas_call(
        gate_kernel,
        in_specs=[VMEM_SPEC] * (1 + len(after)),
        out_specs=VMEM_SPEC,
        out_shape=pltpu.VMEM(sums.shape, jnp.float32),
        input_output_aliases={0: 0},
        compiler_params=pltpu.CompilerParams(vmem_limit_bytes=1 * MIB),
        name="gate",
    )(resident(sums), *(resident(part) for part in after))


def modes_kernel(
    place_ref, scale_ref, level_ref, inv_dr_ref, target_ref, table_ref, edge_ref, near_ref, state_ref,
    sums_ref, tile_ref, behind_ref, rows_ref, axial_ref, swirl_ref, base_ref, split_ref, *, cells, chunk,
):
    step = pl.program_id(0)
    steps = pl.num_programs(0)
    _, planes, columns, cycles = state_ref.shape
    odd = place_ref[0]
    lane = lax.broadcasted_iota(jnp.int32, (chunk, LANES), 1)

    @pl.when(step == 0)
    def _():
        fill_rows(rows_ref, inv_dr_ref[...], 0, cycles, cells)
        for f in range(5):
            axial_ref[0, f] = jnp.where(odd == 1, near_ref[f, :, :LANES], 0.0)
            for i in range(PACK):
                swirl_ref[i, f, 0:8] = jnp.zeros((8, LANES), jnp.float32)
                swirl_ref[i, f, columns + 8 : columns + 16] = jnp.zeros((8, LANES), jnp.float32)

    @pl.when(step > 0)
    def _():
        for f in range(5):
            axial_ref[0, f] = axial_ref[PACK, f]

    def load(plane, start):
        return [state_ref[f, plane, pl.ds(start, chunk), :LANES] for f in range(5)]

    def following(start):
        flux = axial_flux(load(jnp.minimum(step * PACK + PACK, planes - 1), start))
        final = step == steps - 1
        for f in range(5):
            halo = jnp.where(odd == 0, near_ref[f, pl.ds(start, chunk), :LANES], 0.0)
            axial_ref[PACK + 1, f, pl.ds(start, chunk)] = jnp.where(final, halo, flux[f])

    def wide(row):
        return jnp.broadcast_to(row[None], (chunk // 8, 8, LANES)).reshape(chunk, LANES)

    def first(start):
        up, down, around = [wide(rows_ref[k]) for k in range(3)]
        target = [jnp.broadcast_to(target_ref[f : f + 1], (chunk, LANES)) for f in range(5)]
        for i in range(PACK):
            q = load(step * PACK + i, start)
            axial, radial, swirl = all_fluxes(q)
            sponge = level_ref[i, pl.ds(start, chunk), :].astype(jnp.float32) * (time_step * sponge_rate)
            scaled = [around * flux for flux in swirl]
            ahead = [pltpu.roll(flux, LANES - 1, 1) for flux in radial]
            behind = [pltpu.roll(flux, 1, 1) for flux in radial]
            base = base_update(q, sponge, target, ahead, behind, up, down, scaled, cells)
            plane = step * PACK + i
            for f in range(5):
                behind_ref[f, plane, pl.ds(start, chunk)] = behind[f]
                axial_ref[i + 1, f, pl.ds(start, chunk)] = axial[f]
                swirl_ref[i, f, pl.ds(start + 8, chunk)] = scaled[f]
                base_ref[i, f, pl.ds(start, chunk)] = base[f]

    def packed(parts, rows):
        result = parts[0]
        for i in range(1, PACK):
            result = jnp.where(lane[:rows] // CYCLE == i, pltpu.roll(parts[i], i * CYCLE, 1), result)
        return result

    factor = [(0.5 * time_step) * scale_ref[step * PACK + i] for i in range(PACK)]
    total = [jnp.zeros((8, LANES), jnp.float32)] * 5

    def second(start):
        for f in range(5):
            parts = []
            for i in range(PACK):
                value = base_ref[i, f, start : start + chunk]
                value = value - factor[i] * (
                    axial_ref[i + 2, f, start : start + chunk] - axial_ref[i, f, start : start + chunk]
                )
                inside = value + (
                    swirl_ref[i, f, start + 7 : start + 7 + chunk] - swirl_ref[i, f, start + 9 : start + 9 + chunk]
                )
                tile_ref[f, step * PACK + i, start : start + chunk] = inside
                parts.append(inside)
            value = packed(parts, chunk)
            high = value.astype(jnp.bfloat16)
            split_ref[f, start : start + chunk] = high
            split_ref[f, columns + start : columns + start + chunk] = (value - high.astype(jnp.float32)).astype(
                jnp.bfloat16
            )
            total[f] = total[f] + value.reshape(chunk // 8, 8, LANES).sum(axis=0)

    for start in range(0, columns, chunk):
        first(start)
        following(start)
        if start:
            second(start - chunk)
    second(columns - chunk)
    for f in range(5):
        sums = jnp.dot(table_ref[0], split_ref[f], preferred_element_type=jnp.float32)
        half = sums.shape[0] // 2
        start_row = packed([swirl_ref[i, f, 8:16] for i in range(PACK)], 8)[0:1]
        end_row = packed([swirl_ref[i, f, columns : columns + 8] for i in range(PACK)], 8)[7:8]
        group = step * 5 + f
        sums_ref[pl.ds(pl.multiple_of(group * half, half), half), :] = (
            sums[:half] + sums[half:] + (edge_ref[0, 1] * end_row - edge_ref[0, 0] * start_row)
        )
        mean = total[f].sum(axis=0, keepdims=True) + (end_row - start_row)
        sums_ref[pl.ds(steps * 5 * half + group, 1), :] = mean


def mode_rows(planes, half):
    groups = 5 * planes // PACK
    return groups * half + -(-groups // 8) * 8


def inner_modes(place, scale, sponge, inv_dr, target, table, edge, near, state, cells):
    _, planes, columns, cycles = state.shape
    half = table.shape[1] // 2
    chunk = min(32, columns)
    whole = lambda *shape: pl.BlockSpec(shape, lambda g, place: (0,) * len(shape))
    tile = pltpu.VMEM((5, planes, columns, LANES), jnp.float32)
    return pl.pallas_call(
        functools.partial(modes_kernel, cells=cells, chunk=chunk),
        grid_spec=pltpu.PrefetchScalarGridSpec(
            num_scalar_prefetch=1,
            grid=(planes // PACK,),
            in_specs=[
                SMEM_SPEC,
                pl.BlockSpec((PACK, columns, LANES), lambda g, place: (g, 0, 0)),
                whole(1, LANES),
                whole(5, LANES),
                pl.BlockSpec((1,) + table.shape[1:], lambda g, place: (place[1], 0, 0)),
                pl.BlockSpec((1,) + edge.shape[1:], lambda g, place: (place[1], 0, 0, 0)),
                VMEM_SPEC,
                VMEM_SPEC,
            ],
            out_specs=[VMEM_SPEC] * 3,
            scratch_shapes=[
                pltpu.VMEM((3, 8, LANES), jnp.float32),
                pltpu.VMEM((PACK + 2, 5, columns, LANES), jnp.float32),
                pltpu.VMEM((PACK, 5, columns + 16, LANES), jnp.float32),
                pltpu.VMEM((PACK, 5, columns, LANES), jnp.float32),
                pltpu.VMEM((5, 2 * columns, LANES), jnp.bfloat16),
            ],
        ),
        out_shape=[pltpu.VMEM((mode_rows(planes, half), LANES), jnp.float32), tile, tile],
        compiler_params=params(1, 12),
        name="inner_modes",
    )(place, *(stored(part) for part in (scale, sponge, inv_dr, target, table, edge)), resident(near), resident(state))


IN_SLOTS = 3
OUT_SLOTS = 2


def update_kernel(
    place_ref, scale_ref, inv_dr_ref, target_ref, near_ref, halo_ref, behind_ref, state_ref, level_ref,
    out_ref, ahead_ref, kept_ref, rows_ref, levels_ref, result_ref, axial_even_ref, axial_odd_ref, swirl_even_ref,
    swirl_odd_ref, base_ref, level_sem, result_sem, *, cells, chunk, unroll,
):
    axial_refs = (axial_even_ref, axial_odd_ref)
    swirl_refs = (swirl_even_ref, swirl_odd_ref)
    planes, columns, cycles = level_ref.shape
    tiles = cycles // LANES - 1
    odd = place_ref[0]
    rest = pl.ds(LANES, cycles - LANES)
    lane = lax.broadcasted_iota(jnp.int32, (chunk, LANES), 1)

    def fetch(plane):
        slot = lax.rem(plane, IN_SLOTS)
        return pltpu.make_async_copy(level_ref.at[plane, :, rest], levels_ref.at[slot], level_sem.at[slot])

    def store(plane):
        slot = lax.rem(plane, OUT_SLOTS)
        return pltpu.make_async_copy(result_ref.at[slot], out_ref.at[:, plane, :, rest], result_sem.at[slot])

    def keep(plane):
        slot = lax.rem(plane, OUT_SLOTS)
        return pltpu.make_async_copy(result_ref.at[slot], kept_ref, result_sem.at[slot])

    for plane in range(IN_SLOTS):
        fetch(plane).start()

    fill_rows(rows_ref, inv_dr_ref[:, LANES:], LANES, cycles, cells)

    def wide(k, tile):
        row = rows_ref[k, :, tile * LANES : (tile + 1) * LANES]
        return jnp.broadcast_to(row[None], (chunk // 8, 8, LANES)).reshape(chunk, LANES)

    def outside(c, use):
        rows = pl.ds(pl.multiple_of(c * chunk, chunk), chunk)
        return [[jnp.where(use, near_ref[f, rows, (k + 1) * LANES : (k + 2) * LANES], 0.0) for f in range(5)] for k in range(tiles)]

    def before(c, _):
        axial = outside(c, odd == 1)
        for k in range(tiles):
            for f in range(5):
                axial_odd_ref[f, k, pl.ds(pl.multiple_of(c * chunk, chunk), chunk)] = axial[k][f]
        return 0

    lax.fori_loop(0, columns // chunk, before, 0)

    def finish(plane, parity, start, k, axial):
        rows = pl.ds(start, chunk)
        factor = (0.5 * time_step) * scale_ref[jnp.maximum(plane - 1, 0)]
        axial_ref, swirl_ref = axial_refs[parity], swirl_refs[1 - parity]
        slot = lax.rem(plane + OUT_SLOTS - 1, OUT_SLOTS)
        for f in range(5):
            value = base_ref[f, k, rows] - factor * (axial[f] - axial_ref[f, k, rows])
            value = value + (
                swirl_ref[f, k, pl.ds(start + 7, chunk)] - swirl_ref[f, k, pl.ds(start + 9, chunk)]
            )
            result_ref[slot, f, rows, k * LANES : (k + 1) * LANES] = value

    def one_chunk(plane, parity, c):
        start = pl.multiple_of(c * chunk, chunk)
        rows = pl.ds(start, chunk)
        slot = lax.rem(plane, IN_SLOTS)

        def open_tile(k):
            q = [state_ref[f, plane, rows, (k + 1) * LANES : (k + 2) * LANES] for f in range(5)]
            axial, radial, swirl = all_fluxes(q)
            ahead = [pltpu.roll(flux, LANES - 1, 1) for flux in radial]
            behind = [pltpu.roll(flux, 1, 1) for flux in radial]
            return q, axial, swirl, ahead, behind

        def close_tile(k, last, this, following):
            q, axial, swirl, ahead, behind = this
            if following is not None:
                ahead = [jnp.where(lane == LANES - 1, following[3][f], ahead[f]) for f in range(5)]
            if last is not None:
                first = last[4]
            else:
                first = [behind_ref[f, plane, rows] for f in range(5)]
                for f in range(5):
                    ahead_ref[f, plane, rows] = this[3][f]
            behind = [jnp.where(lane == 0, first[f], behind[f]) for f in range(5)]
            sponge = levels_ref[slot, rows, k * LANES : (k + 1) * LANES].astype(jnp.float32) * (
                time_step * sponge_rate
            )
            target = [
                jnp.broadcast_to(target_ref[f : f + 1, (k + 1) * LANES : (k + 2) * LANES], (chunk, LANES))
                for f in range(5)
            ]
            around = wide(2, k)
            scaled = [around * flux for flux in swirl]
            base = base_update(q, sponge, target, ahead, behind, wide(0, k), wide(1, k), scaled, cells)
            finish(plane, parity, start, k, axial)
            for f in range(5):
                base_ref[f, k, rows] = base[f]
                axial_refs[parity][f, k, rows] = axial[f]
                swirl_refs[parity][f, k, pl.ds(start + 8, chunk)] = scaled[f]

        opened = [open_tile(0)]
        for k in range(tiles):
            if k + 1 < tiles:
                opened.append(open_tile(k + 1))
            close_tile(
                k, opened[k - 1] if k else None, opened[k], opened[k + 1] if k + 1 < tiles else None
            )

    def one_plane(plane, parity):
        fetch(plane).wait()
        for f in range(5):
            for side, row in ((0, 7), (1, columns + 8)):
                edge = halo_ref[side, f, pl.ds(plane, 1), :]
                for k in range(tiles):
                    around = rows_ref[2, 0:1, k * LANES : (k + 1) * LANES]
                    swirl_refs[parity][f, k, row : row + 1] = around * edge[:, (k + 1) * LANES : (k + 2) * LANES]
        pl.when(plane > OUT_SLOTS)(lambda: store(plane - 1 - OUT_SLOTS).wait())

        def step(c, _):
            one_chunk(plane, parity, c)
            return 0

        lax.fori_loop(0, columns // chunk, step, 0, unroll=unroll)
        outer = jnp.logical_and(plane == 1, odd == 0)
        pl.when(outer)(lambda: keep(plane - 1).start())
        pl.when(jnp.logical_and(plane > 0, jnp.logical_not(outer)))(lambda: store(plane - 1).start())

        @pl.when(plane + IN_SLOTS < planes)
        def _():
            fetch(plane + IN_SLOTS).start()

    def two_planes(pair, _):
        for parity in range(2):
            one_plane(2 * pair + parity, parity)
        return 0

    lax.fori_loop(0, planes // 2, two_planes, 0)
    store(planes - 1 - OUT_SLOTS).wait()

    def last(c, _):
        start = pl.multiple_of(c * chunk, chunk)
        axial = outside(c, odd == 0)
        for k in range(tiles):
            finish(planes, 0, start, k, axial[k])
        return 0

    lax.fori_loop(0, columns // chunk, last, 0)
    pl.when(odd == 0)(lambda: store(planes - 1).start())
    pl.when(odd == 1)(lambda: keep(planes - 1).start())
    for plane in range(planes - OUT_SLOTS, planes):
        store(plane).wait()


def bulk_update(place, scale, state, sponge, inv_dr, target, near, halo, behind, cells, chunk=8, unroll=16):
    _, planes, columns, cycles = state.shape
    tiles = cycles // LANES - 1
    width = cycles - LANES
    return pl.pallas_call(
        functools.partial(update_kernel, cells=cells, chunk=chunk, unroll=unroll),
        in_specs=[SMEM_SPEC, SMEM_SPEC, VMEM_SPEC, VMEM_SPEC, VMEM_SPEC, VMEM_SPEC, VMEM_SPEC, VMEM_SPEC, HBM_SPEC],
        out_specs=[HBM_SPEC, VMEM_SPEC, VMEM_SPEC],
        scratch_shapes=[
            pltpu.VMEM((3, 8, width), jnp.float32),
            pltpu.VMEM((IN_SLOTS, columns, width), jnp.int32),
            pltpu.VMEM((OUT_SLOTS, 5, columns, width), jnp.float32),
            pltpu.VMEM((5, tiles, columns, LANES), jnp.float32),
            pltpu.VMEM((5, tiles, columns, LANES), jnp.float32),
            pltpu.VMEM((5, tiles, columns + 16, LANES), jnp.float32),
            pltpu.VMEM((5, tiles, columns + 16, LANES), jnp.float32),
            pltpu.VMEM((5, tiles, columns, LANES), jnp.float32),
            pltpu.SemaphoreType.DMA((IN_SLOTS,)),
            pltpu.SemaphoreType.DMA((OUT_SLOTS,)),
        ],
        out_shape=[
            jax.ShapeDtypeStruct(state.shape, jnp.float32),
            pltpu.VMEM((5, planes, columns, LANES), jnp.float32),
            pltpu.VMEM((5, columns, width), jnp.float32),
        ],
        compiler_params=pltpu.CompilerParams(vmem_limit_bytes=13 * MIB),
        input_output_aliases={6: 1},
        name="bulk_update",
    )(place, scale, inv_dr, target, resident(near), resident(halo), resident(behind), resident(state), stored(sponge))


def filter_kernel(
    place_ref, cutoff_ref, table_ref, inv_dr_ref, tile_ref, ahead_ref, halo_ref, *refs, cells, cycles
):
    *sums, state_ref, out_ref, kept_ref, split_ref = refs
    step = pl.program_id(0)
    steps = pl.num_programs(0)
    half = table_ref.shape[2] // 4
    columns = out_ref.shape[2]
    weight = mode_weight(cutoff_ref[...], half, cells)
    lane = lax.broadcasted_iota(jnp.int32, (columns, LANES), 1)
    spacing = 4.0 / cycles
    edge = 1.0 + spacing * (LANES - 1)
    up = (0.5 * time_step) * inv_dr_ref[...] * ((edge + spacing) / edge)
    up = jnp.where(lane == LANES - 1, up, 0.0)
    cycle = lax.broadcasted_iota(jnp.int32, (1, LANES), 1)
    around = (time_step * cells / (4.0 * math.pi)) / (1.0 + spacing * cycle.astype(jnp.float32))
    around = jnp.where(cycle < CYCLE, 0.0, around)
    for f in range(5):
        group = step * 5 + f
        values = turn_back(
            sums, pl.multiple_of(group * half, half), steps * 5 * half + group, weight, table_ref[0],
            split_ref.at[f], cells,
        )
        for i in range(PACK):
            turned = values if i == 0 else pltpu.roll(values, LANES - i * CYCLE, 1)
            plane = step * PACK + i
            out_ref[f, i] = jnp.where(lane < CYCLE, turned, tile_ref[f, plane] - up * ahead_ref[f, plane])
            low = halo_ref[0, f, pl.ds(plane, 1), :][:, :LANES]
            high = halo_ref[1, f, pl.ds(plane, 1), :][:, :LANES]
            out_ref[f, i, 0:1] = out_ref[f, i, 0:1] + around * low
            out_ref[f, i, columns - 1 : columns] = out_ref[f, i, columns - 1 : columns] - around * high

    def keep(i):
        for f in range(5):
            kept_ref[f] = out_ref[f, i]

    odd = place_ref[0]
    pl.when(jnp.logical_and(step == 0, odd == 0))(lambda: keep(0))
    pl.when(jnp.logical_and(step == steps - 1, odd == 1))(lambda: keep(PACK - 1))


def put_filtered(place, cutoff, table, inv_dr, tile, ahead, halo, sums, updated, cells):
    _, planes, columns, cycles = updated.shape
    return pl.pallas_call(
        functools.partial(filter_kernel, cells=cells, cycles=cycles),
        grid_spec=pltpu.PrefetchScalarGridSpec(
            num_scalar_prefetch=1,
            grid=(planes // PACK,),
            in_specs=[
                pl.BlockSpec(cutoff.shape, lambda g, place: (0, 0)),
                pl.BlockSpec((1,) + table.shape[1:], lambda g, place: (place[1], 0, 0)),
                pl.BlockSpec((1, LANES), lambda g, place: (0, 0)),
                VMEM_SPEC,
                VMEM_SPEC,
                VMEM_SPEC,
            ]
            + [VMEM_SPEC] * len(sums)
            + [HBM_SPEC],
            out_specs=[pl.BlockSpec((5, PACK, columns, LANES), lambda g, place: (0, g, 0, 0)), VMEM_SPEC],
            scratch_shapes=[pltpu.VMEM((5, table.shape[2], LANES), jnp.bfloat16)],
        ),
        out_shape=[
            jax.ShapeDtypeStruct(updated.shape, jnp.float32),
            pltpu.VMEM((5, columns, LANES), jnp.float32),
        ],
        input_output_aliases={7 + len(sums): 0},
        compiler_params=params(1, 12),
        name="put_filtered",
    )(place, cutoff, table, inv_dr, resident(tile), resident(ahead), resident(halo),
      *(resident(part) for part in sums), updated)


def outer_kernel(place_ref, scale_ref, table_ref, flux_ref, after_ref, sums_ref, split_ref):
    odd = place_ref[0]
    planes = scale_ref.shape[0]
    columns = flux_ref.shape[1]
    half = table_ref.shape[1] // 2
    factor = (0.5 * time_step) * scale_ref[odd * (planes - 1)]
    factor = jnp.where(odd == 1, -factor, factor)
    lane = lax.broadcasted_iota(jnp.int32, (columns, LANES), 1)
    for group in range(2):
        value = jnp.zeros((columns, LANES), jnp.float32)
        for i in range(PACK):
            if group * PACK + i < 5:
                part = factor * flux_ref[group * PACK + i, :, :LANES]
                part = part if i == 0 else pltpu.roll(part, i * CYCLE, 1)
                value = jnp.where(lane // CYCLE == i, part, value)
        high = value.astype(jnp.bfloat16)
        split_ref[group, :columns] = high
        split_ref[group, columns:] = (value - high.astype(jnp.float32)).astype(jnp.bfloat16)
        sums = jnp.dot(table_ref[place_ref[1]], split_ref[group], preferred_element_type=jnp.float32)
        sums_ref[group * half : (group + 1) * half] = sums[:half] + sums[half:]
        sums_ref[2 * half + group : 2 * half + group + 1] = value.sum(axis=0, keepdims=True)


def outer_modes(place, scale, table, flux, after):
    half = table.shape[1] // 2
    return pl.pallas_call(
        outer_kernel,
        in_specs=[SMEM_SPEC, SMEM_SPEC, VMEM_SPEC, VMEM_SPEC, VMEM_SPEC],
        out_specs=VMEM_SPEC,
        scratch_shapes=[pltpu.VMEM((2, 2 * flux.shape[1], LANES), jnp.bfloat16)],
        out_shape=pltpu.VMEM((2 * half + 8, LANES), jnp.float32),
        compiler_params=pltpu.CompilerParams(vmem_limit_bytes=4 * MIB),
        name="outer_modes",
    )(place, scale, table, resident(flux), resident(after))


def turn_back(sums, base, mean_row, weight, table, split_ref, cells):
    half = weight.shape[0]
    coefficient = sums[0][pl.ds(base, half), :]
    mean = sums[0][pl.ds(mean_row, 1), :]
    for other in sums[1:]:
        coefficient = coefficient + other[pl.ds(base, half), :]
        mean = mean + other[pl.ds(mean_row, 1), :]
    coefficient = coefficient * weight
    high = coefficient.astype(jnp.bfloat16)
    low = (coefficient - high.astype(jnp.float32)).astype(jnp.bfloat16)
    for k in range(2):
        split_ref[2 * k * half : (2 * k + 1) * half] = high
        split_ref[(2 * k + 1) * half : (2 * k + 2) * half] = low
    return jnp.dot(table, split_ref[...], preferred_element_type=jnp.float32) + mean * (1.0 / cells)


def mode_weight(cutoff, half, cells):
    count = half // 2
    mode = lax.broadcasted_iota(jnp.int32, (half, LANES), 0)
    mode = jnp.where(mode >= count, mode - count, mode) + 1
    return jnp.where(mode <= jnp.concatenate([cutoff] * PACK, axis=1), 2.0 / cells, 0.0)


def finish_kernel(place_ref, scale_ref, cutoff_ref, table_ref, flux_ref, first_ref, rest_ref, *refs, cells):
    *sums, state_ref, out_ref, result_ref, split_ref, result_sem = refs
    odd = place_ref[0]
    planes = scale_ref.shape[0]
    columns = flux_ref.shape[1]
    half = table_ref.shape[2] // 4
    plane = odd * (planes - 1)
    factor = (0.5 * time_step) * scale_ref[plane]
    factor = jnp.where(odd == 1, -factor, factor)
    lane = lax.broadcasted_iota(jnp.int32, (columns, LANES), 1)
    weight = mode_weight(cutoff_ref[...], half, cells)
    table = table_ref[place_ref[1]]
    copies = []
    for f in range(5):
        group, i = f // PACK, f % PACK
        if i == 0:
            values = turn_back(sums, group * half, 2 * half + group, weight, table, split_ref.at[group], cells)
        turned = values if i == 0 else pltpu.roll(values, LANES - i * CYCLE, 1)
        flux = factor * flux_ref[f]
        result_ref[f, :, :LANES] = first_ref[f] + jnp.where(lane < CYCLE, turned, flux[:, :LANES])
        result_ref[f, :, LANES:] = rest_ref[f] + flux[:, LANES:]
        copies.append(pltpu.make_async_copy(result_ref.at[f], out_ref.at[f, plane], result_sem.at[f]))
        copies[-1].start()
    for copy in copies:
        copy.wait()


def finish_plane(place, scale, cutoff, table, flux, first, rest, sums, updated, cells):
    return pl.pallas_call(
        functools.partial(finish_kernel, cells=cells),
        in_specs=[SMEM_SPEC, SMEM_SPEC] + [VMEM_SPEC] * (5 + len(sums)) + [HBM_SPEC],
        out_specs=HBM_SPEC,
        scratch_shapes=[
            pltpu.VMEM(flux.shape, jnp.float32),
            pltpu.VMEM((2, table.shape[2], LANES), jnp.bfloat16),
            pltpu.SemaphoreType.DMA((5,)),
        ],
        out_shape=jax.ShapeDtypeStruct(updated.shape, jnp.float32),
        input_output_aliases={7 + len(sums): 0},
        compiler_params=pltpu.CompilerParams(vmem_limit_bytes=4 * MIB),
        name="finish_plane",
    )(
        place, scale, cutoff, table, resident(flux), resident(first), resident(rest),
        *(resident(part) for part in sums), updated,
    )


def mode_tables(cells, sectors):
    columns = cells // sectors
    mode = np.arange(1, cells // 8 + 1)

    def waves(cell):
        angle = 2.0 * np.pi / cells * ((mode[:, None] * cell[None, :]) % cells)
        return np.concatenate([np.cos(angle), np.sin(angle)])

    forward, inverse, edge = [], [], []
    for sector in range(sectors):
        wave = waves(sector * columns + np.arange(columns))
        high = wave.astype(ml_dtypes.bfloat16)
        low = (wave - high.astype(np.float64)).astype(ml_dtypes.bfloat16)
        forward.append(np.block([[high, high], [low, low]]))
        inverse.append(np.concatenate([high.T, high.T, low.T, low.T], axis=1))
        ends = waves(np.array([sector * columns - 1, (sector + 1) * columns]) % cells)
        edge.append(np.broadcast_to(ends.T[:, :, None], (2, ends.shape[0], LANES)))
    return np.stack(forward), np.stack(inverse), np.stack(edge).astype(np.float32)


def body(forward, inverse, edge, cells, state, sponge_level, inv_dx, inv_dr, target, cutoff):
    sectors = lax.axis_size("az")
    rows = lax.axis_size("gx")
    place = jnp.stack([lax.rem(lax.axis_index("gx"), 2), lax.axis_index("az")]).astype(jnp.int32)
    cycles = state.shape[3]
    inv_dr = inv_dr.reshape(1, cycles)
    cutoff = cutoff.reshape(1, CYCLE)

    near_pairs = [(i ^ 1, i) for i in range(rows) if i ^ 1 < rows]
    far_pairs = [(i, i + 1) for i in range(1, rows - 1, 2)] + [(i + 1, i) for i in range(1, rows - 1, 2)]
    shifted = lambda part, by: lax.ppermute(part, "az", [(i, (i + by) % sectors) for i in range(sectors)])

    edges, far_flux, near_flux = edge_cells(place, stored(state))
    far_flux = lax.ppermute(far_flux, "gx", far_pairs)
    near_flux = lax.ppermute(near_flux, "gx", near_pairs)
    if sectors == 2:
        halo = shifted(edges, 1)
    else:
        halo = jnp.stack([shifted(edges[0], 1), shifted(edges[1], sectors - 1)])
    sums, tile, behind = inner_modes(
        place, inv_dx, sponge_level, inv_dr, target, forward, edge, near_flux, state, cells
    )
    sums = gate(sums, [halo])
    others = [shifted(sums, by) for by in range(1, sectors)]
    updated, ahead, rest = bulk_update(
        place, inv_dx, state, sponge_level, inv_dr, target, near_flux, halo, behind, cells
    )
    outer = outer_modes(place, inv_dx, forward, far_flux, rest)
    outer = [outer] + [shifted(outer, by) for by in range(1, sectors)]
    updated, first = put_filtered(place, cutoff, inverse, inv_dr, tile, ahead, halo, [sums, *others], updated, cells)
    return finish_plane(place, inv_dx, cutoff, inverse, far_flux, first, rest, outer, updated, cells)


def solution(mesh):
    def whole(state, sponge_level, inv_dx, inv_dr, target, cutoff):
        cells = state.shape[2]
        tables = mode_tables(cells, mesh.shape["az"])
        mapped = jax.shard_map(
            functools.partial(body, *(jnp.asarray(table) for table in tables), cells),
            mesh=mesh,
            in_specs=(P(None, "gx", "az", None), P("gx", "az", None), P("gx"), P(), P(), P()),
            out_specs=P(None, "gx", "az", None),
            check_vma=False,
        )
        return mapped(state, sponge_level, inv_dx, inv_dr, target, cutoff)

    return whole
```

```python
import functools
import math

import jax
import jax.numpy as jnp
import ml_dtypes
import numpy as np
from jax import lax
from jax.experimental import pallas as pl
from jax.experimental.pallas import tpu as pltpu
from jax.sharding import PartitionSpec as P

CYCLE = 32
LANES = 128
PACK = LANES // CYCLE

gas_factor = 0.4
time_step = 0.02
sponge_rate = 4.0

MIB = 1024 * 1024


def params(steps, limit):
    return pltpu.CompilerParams(
        dimension_semantics=("arbitrary",) * steps, vmem_limit_bytes=limit * MIB
    )


def place():
    return lax.rem(lax.axis_index("gx"), 2), lax.axis_index("az")


def stored(x):
    return pltpu.with_memory_space_constraint(x, pltpu.HBM)


def resident(x):
    return pltpu.with_memory_space_constraint(x, pltpu.VMEM)


VMEM_SPEC = pl.BlockSpec(memory_space=pltpu.VMEM)
SMEM_SPEC = pl.BlockSpec(memory_space=pltpu.SMEM)
HBM_SPEC = pl.BlockSpec(memory_space=pl.ANY)


def products(q):
    density, m, n, s, energy = q
    inverse = pltpu.reciprocal(density, approx=True)
    u, v, w = m * inverse, n * inverse, s * inverse
    mu, nv, sw = m * u, n * v, s * w
    pressure = gas_factor * energy - (0.5 * gas_factor) * (mu + nv + sw)
    return u, v, w, mu, nv, sw, pressure, energy + pressure


def axial_flux(q):
    u, _, _, mu, _, _, pressure, enthalpy = products(q)
    return (q[1], mu + pressure, q[2] * u, q[3] * u, enthalpy * u)


def swirl_flux(q):
    _, _, w, _, _, sw, pressure, enthalpy = products(q)
    return (q[3], q[1] * w, q[2] * w, sw + pressure, enthalpy * w)


def all_fluxes(q):
    u, v, w, mu, nv, sw, pressure, enthalpy = products(q)
    mv, mw, nw = q[1] * v, q[1] * w, q[2] * w
    axial = (q[1], mu + pressure, mv, mw, enthalpy * u)
    radial = (q[2], mv, nv + pressure, nw, enthalpy * v)
    swirl = (q[3], mw, nw, sw + pressure, enthalpy * w)
    return axial, radial, swirl


def fill_rows(rows_ref, inv_dr, start, cycles, cells):
    width = rows_ref.shape[-1]
    cycle = lax.broadcasted_iota(jnp.int32, (8, width), 1) + start
    spacing = 4.0 / cycles
    radius = 1.0 + spacing * cycle.astype(jnp.float32)
    inverse = 1.0 / radius
    half = (0.5 * time_step) * jnp.broadcast_to(inv_dr, (8, width)) * inverse
    rows_ref[0] = jnp.where(cycle == start + width - 1, 0.0, half * (radius + spacing))
    rows_ref[1] = jnp.where(cycle == 0, 0.0, half * (radius - spacing))
    rows_ref[2] = (time_step * cells / (4.0 * math.pi)) * inverse


def base_update(q, sponge, target, ahead, behind, up, down, scaled, cells):
    source = 4.0 * math.pi / cells
    result = []
    for f in range(5):
        value = q[f] - sponge * (q[f] - target[f]) - (up * ahead[f] - down * behind[f])
        if f == 2:
            value = value + source * scaled[3]
        if f == 3:
            value = value - source * scaled[2]
        result.append(value)
    return result


PARTS = 2


def plane_copies(state_ref, plane, plane_ref, sem):
    rows = state_ref.shape[2] // PARTS
    return [
        pltpu.make_async_copy(
            state_ref.at[:, plane, pl.ds(part * rows, rows)], plane_ref.at[:, pl.ds(part * rows, rows)], sem.at[part]
        )
        for part in range(PARTS)
    ]


def edge_kernel(
    state_ref, scale_ref, edge_ref, first_ref, rest_ref, near_ref, factor_ref, row_ref, far_plane_ref, near_plane_ref,
    held_ref, row_sem, plane_sem, held_sem,
):
    _, planes, columns, cycles = state_ref.shape
    odd, _ = place()
    scales = pltpu.make_async_copy(scale_ref, held_ref, held_sem.at[0])
    ends = [
        pltpu.make_async_copy(
            state_ref.at[:, :, pl.ds(side * (columns - 1), 1)], row_ref.at[side], row_sem.at[side]
        )
        for side in range(2)
    ]
    far = plane_copies(state_ref, odd * (planes - 1), far_plane_ref, plane_sem.at[0])
    near = plane_copies(state_ref, (1 - odd) * (planes - 1), near_plane_ref, plane_sem.at[1])
    for copy in far + near + ends + [scales]:
        copy.start()
    rows = columns // PARTS
    for part, copy in enumerate(far):
        copy.wait()
        cut = slice(part * rows, (part + 1) * rows)
        flux = axial_flux([far_plane_ref[f, cut] for f in range(5)])
        for f in range(5):
            first_ref[f, cut] = flux[f][:, :LANES]
            rest_ref[f, cut] = flux[f][:, LANES:]
    for part, copy in enumerate(near):
        copy.wait()
        cut = slice(part * rows, (part + 1) * rows)
        flux = axial_flux([near_plane_ref[f, cut] for f in range(5)])
        for f in range(5):
            near_ref[f, cut] = flux[f]
    for copy in ends:
        copy.wait()
    for side in range(2):
        flux = swirl_flux([row_ref[1 - side, f, :, 0, :] for f in range(5)])
        for f in range(5):
            edge_ref[side, f] = flux[f]
    scales.wait()
    for plane in range(planes):
        factor_ref[plane] = jnp.full((8, LANES), (0.5 * time_step) * held_ref[plane], jnp.float32)


def edge_cells(state, scale):
    _, planes, columns, cycles = state.shape
    plane = pltpu.VMEM((5, columns, cycles), jnp.float32)
    return pl.pallas_call(
        edge_kernel,
        in_specs=[HBM_SPEC, HBM_SPEC],
        out_specs=[VMEM_SPEC] * 5,
        scratch_shapes=[
            pltpu.VMEM((2, 5, planes, 1, cycles), jnp.float32),
            plane,
            plane,
            pltpu.SMEM(scale.shape, jnp.float32),
            pltpu.SemaphoreType.DMA((2,)),
            pltpu.SemaphoreType.DMA((2, PARTS)),
            pltpu.SemaphoreType.DMA((1,)),
        ],
        out_shape=[
            pltpu.VMEM((2, 5, planes, cycles), jnp.float32),
            pltpu.VMEM((5, columns, LANES), jnp.float32),
            pltpu.VMEM((5, columns, cycles - LANES), jnp.float32),
            plane,
            pltpu.VMEM((planes, 8, LANES), jnp.float32),
        ],
        compiler_params=pltpu.CompilerParams(vmem_limit_bytes=6 * MIB),
        name="edge_cells",
    )(stored(state), stored(scale))


def gate_kernel(flux_ref, after_ref, out_ref):
    out_ref[0, 0:8, 0:LANES] = flux_ref[0, 0:8, 0:LANES]


def gate(flux, after):
    return pl.pallas_call(
        gate_kernel,
        in_specs=[VMEM_SPEC, VMEM_SPEC],
        out_specs=VMEM_SPEC,
        out_shape=pltpu.VMEM(flux.shape, jnp.float32),
        input_output_aliases={0: 0},
        compiler_params=pltpu.CompilerParams(vmem_limit_bytes=1 * MIB),
        name="gate",
    )(resident(flux), resident(after))


def modes_kernel(
    level_ref, inv_dr_ref, target_ref, factor_ref, table_ref, edge_ref, state_ref, *refs,
    cells, chunk, pick, steps, ends,
):
    sums_ref, tile_ref, behind_ref, rows_ref, axial_ref, swirl_ref, base_ref, split_ref = refs[-8:]
    step = pick(pl.program_id(0))
    _, planes, columns, cycles = state_ref.shape
    odd, sector = place()
    lane = lax.broadcasted_iota(jnp.int32, (chunk, LANES), 1)

    @pl.when(pl.program_id(0) == 0)
    def _():
        fill_rows(rows_ref, inv_dr_ref[...], 0, cycles, cells)
        for f in range(5):
            for i in range(PACK):
                swirl_ref[i, f, 0:8] = jnp.zeros((8, LANES), jnp.float32)
                swirl_ref[i, f, columns + 8 : columns + 16] = jnp.zeros((8, LANES), jnp.float32)

    def load(plane, start):
        return [state_ref[f, plane, pl.ds(start, chunk), :LANES] for f in range(5)]

    def beside(start):
        for slot, plane, at_end, use in (
            (0, step * PACK - 1, step == 0, odd == 1),
            (PACK + 1, step * PACK + PACK, step == steps - 1, odd == 0),
        ):
            flux = axial_flux(load(jnp.clip(plane, 0, planes - 1), start))
            for f in range(5):
                value = flux[f]
                if ends:
                    halo = jnp.where(use, refs[0][f, pl.ds(start, chunk), :LANES], refs[1][f, pl.ds(start, chunk)])
                    value = jnp.where(at_end, halo, value)
                axial_ref[slot, f, pl.ds(start, chunk)] = value

    def wide(row):
        return jnp.broadcast_to(row[None], (chunk // 8, 8, LANES)).reshape(chunk, LANES)

    def first(start):
        up, down, around = [wide(rows_ref[k]) for k in range(3)]
        target = [jnp.broadcast_to(target_ref[f : f + 1], (chunk, LANES)) for f in range(5)]
        for i in range(PACK):
            q = load(step * PACK + i, start)
            axial, radial, swirl = all_fluxes(q)
            sponge = level_ref[i, pl.ds(start, chunk), :].astype(jnp.float32) * (time_step * sponge_rate)
            scaled = [around * flux for flux in swirl]
            ahead = [pltpu.roll(flux, LANES - 1, 1) for flux in radial]
            behind = [pltpu.roll(flux, 1, 1) for flux in radial]
            base = base_update(q, sponge, target, ahead, behind, up, down, scaled, cells)
            plane = step * PACK + i
            for f in range(5):
                behind_ref[f, plane, pl.ds(start, chunk)] = behind[f]
                axial_ref[i + 1, f, pl.ds(start, chunk)] = axial[f]
                swirl_ref[i, f, pl.ds(start + 8, chunk)] = scaled[f]
                base_ref[i, f, pl.ds(start, chunk)] = base[f]

    def packed(parts, rows):
        result = parts[0]
        for i in range(1, PACK):
            result = jnp.where(lane[:rows] // CYCLE == i, pltpu.roll(parts[i], i * CYCLE, 1), result)
        return result

    factor = [wide(factor_ref[step * PACK + i]) for i in range(PACK)]
    total = [jnp.zeros((8, LANES), jnp.float32)] * 5

    def second(start):
        for f in range(5):
            parts = []
            for i in range(PACK):
                value = base_ref[i, f, start : start + chunk]
                value = value - factor[i] * (
                    axial_ref[i + 2, f, start : start + chunk] - axial_ref[i, f, start : start + chunk]
                )
                inside = value + (
                    swirl_ref[i, f, start + 7 : start + 7 + chunk] - swirl_ref[i, f, start + 9 : start + 9 + chunk]
                )
                tile_ref[f, step * PACK + i, start : start + chunk] = inside
                parts.append(inside)
            value = packed(parts, chunk)
            high = value.astype(jnp.bfloat16)
            split_ref[f, start : start + chunk] = high
            split_ref[f, columns + start : columns + start + chunk] = (value - high.astype(jnp.float32)).astype(
                jnp.bfloat16
            )
            total[f] = total[f] + value.reshape(chunk // 8, 8, LANES).sum(axis=0)

    for start in range(0, columns, chunk):
        first(start)
        beside(start)
        if start:
            second(start - chunk)
    second(columns - chunk)
    for f in range(5):
        sums = jnp.dot(table_ref[sector], split_ref[f], preferred_element_type=jnp.float32)
        half = sums.shape[0] // 2
        start_row = packed([swirl_ref[i, f, 8:16] for i in range(PACK)], 8)[0:1]
        end_row = packed([swirl_ref[i, f, columns : columns + 8] for i in range(PACK)], 8)[7:8]
        group = step * 5 + f
        sums_ref[pl.ds(pl.multiple_of(group * half, half), half), :] = (
            sums[:half] + sums[half:] + (edge_ref[sector, 1] * end_row - edge_ref[sector, 0] * start_row)
        )
        mean = total[f].sum(axis=0, keepdims=True) + (end_row - start_row)
        sums_ref[pl.ds(steps * 5 * half + group, 1), :] = mean


def mode_rows(planes, half):
    groups = 5 * planes // PACK
    return groups * half + -(-groups // 8) * 8


def inner_modes(sponge, inv_dr, target, factor, table, edge, state, cells, near=None, far=None, after=None, done=()):
    _, planes, columns, cycles = state.shape
    half = table.shape[1] // 2
    chunk = min(16, columns)
    steps = planes // PACK
    ends = bool(done)
    pick = (lambda g: g * (steps - 1)) if ends else (lambda g: g + 1)
    whole = lambda *shape: pl.BlockSpec(shape, lambda g: (0,) * len(shape))
    tile = pltpu.VMEM((5, planes, columns, LANES), jnp.float32)
    extra = [resident(part) for part in ((near, far, after) + tuple(done) if ends else ())]
    return pl.pallas_call(
        functools.partial(modes_kernel, cells=cells, chunk=chunk, pick=pick, steps=steps, ends=ends),
        grid=(2 if ends else steps - 2,),
        in_specs=[
            pl.BlockSpec((PACK, columns, LANES), lambda g: (pick(g), 0, 0)),
            whole(1, LANES),
            whole(5, LANES),
            VMEM_SPEC,
            whole(*table.shape),
            whole(*edge.shape),
            VMEM_SPEC,
        ]
        + [VMEM_SPEC] * len(extra),
        out_specs=[VMEM_SPEC, VMEM_SPEC, VMEM_SPEC],
        scratch_shapes=[
            pltpu.VMEM((3, 8, LANES), jnp.float32),
            pltpu.VMEM((PACK + 2, 5, columns, LANES), jnp.float32),
            pltpu.VMEM((PACK, 5, columns + 16, LANES), jnp.float32),
            pltpu.VMEM((PACK, 5, columns, LANES), jnp.float32),
            pltpu.VMEM((5, 2 * columns, LANES), jnp.bfloat16),
        ],
        out_shape=[pltpu.VMEM((mode_rows(planes, half), LANES), jnp.float32), tile, tile],
        input_output_aliases={10 + k: k for k in range(3)} if ends else {},
        compiler_params=params(1, 8),
        name="end_modes" if ends else "middle_modes",
    )(
        *(stored(part) for part in (sponge, inv_dr, target)), resident(factor), stored(table), stored(edge),
        resident(state), *extra,
    )


IN_SLOTS = 3
OUT_SLOTS = 2


def update_kernel(
    inv_dr_ref, target_ref, factor_ref, near_ref, halo_ref, behind_ref, state_ref, level_ref,
    out_ref, ahead_ref, kept_ref, rows_ref, levels_ref, result_ref, axial_even_ref, axial_odd_ref, swirl_even_ref,
    swirl_odd_ref, base_ref, level_sem, result_sem, *, cells, chunk, unroll,
):
    axial_refs = (axial_even_ref, axial_odd_ref)
    swirl_refs = (swirl_even_ref, swirl_odd_ref)
    planes, columns, cycles = level_ref.shape
    tiles = cycles // LANES - 1
    odd, _ = place()
    rest = pl.ds(LANES, cycles - LANES)
    lane = lax.broadcasted_iota(jnp.int32, (chunk, LANES), 1)

    def fetch(plane):
        slot = lax.rem(plane, IN_SLOTS)
        return pltpu.make_async_copy(level_ref.at[plane, :, rest], levels_ref.at[slot], level_sem.at[slot])

    def store(plane):
        slot = lax.rem(plane, OUT_SLOTS)
        return pltpu.make_async_copy(result_ref.at[slot], out_ref.at[:, plane, :, rest], result_sem.at[slot])

    def keep(plane):
        slot = lax.rem(plane, OUT_SLOTS)
        return pltpu.make_async_copy(result_ref.at[slot], kept_ref, result_sem.at[slot])

    for plane in range(IN_SLOTS):
        fetch(plane).start()

    fill_rows(rows_ref, inv_dr_ref[:, LANES:], LANES, cycles, cells)

    def wide(k, tile):
        row = rows_ref[k, :, tile * LANES : (tile + 1) * LANES]
        return jnp.broadcast_to(row[None], (chunk // 8, 8, LANES)).reshape(chunk, LANES)

    def outside(c, use):
        rows = pl.ds(pl.multiple_of(c * chunk, chunk), chunk)
        return [[jnp.where(use, near_ref[f, rows, (k + 1) * LANES : (k + 2) * LANES], 0.0) for f in range(5)] for k in range(tiles)]

    def before(c, _):
        axial = outside(c, odd == 1)
        for k in range(tiles):
            for f in range(5):
                axial_odd_ref[f, k, pl.ds(pl.multiple_of(c * chunk, chunk), chunk)] = axial[k][f]
        return 0

    lax.fori_loop(0, columns // chunk, before, 0)

    def finish(plane, parity, start, k, axial):
        rows = pl.ds(start, chunk)
        factor = factor_ref[jnp.maximum(plane - 1, 0)]
        factor = jnp.broadcast_to(factor[None], (chunk // 8, 8, LANES)).reshape(chunk, LANES)
        axial_ref, swirl_ref = axial_refs[parity], swirl_refs[1 - parity]
        slot = lax.rem(plane + OUT_SLOTS - 1, OUT_SLOTS)
        for f in range(5):
            value = base_ref[f, k, rows] - factor * (axial[f] - axial_ref[f, k, rows])
            value = value + (
                swirl_ref[f, k, pl.ds(start + 7, chunk)] - swirl_ref[f, k, pl.ds(start + 9, chunk)]
            )
            result_ref[slot, f, rows, k * LANES : (k + 1) * LANES] = value

    def one_chunk(plane, parity, c):
        start = pl.multiple_of(c * chunk, chunk)
        rows = pl.ds(start, chunk)
        slot = lax.rem(plane, IN_SLOTS)

        def open_tile(k):
            q = [state_ref[f, plane, rows, (k + 1) * LANES : (k + 2) * LANES] for f in range(5)]
            axial, radial, swirl = all_fluxes(q)
            ahead = [pltpu.roll(flux, LANES - 1, 1) for flux in radial]
            behind = [pltpu.roll(flux, 1, 1) for flux in radial]
            return q, axial, swirl, ahead, behind

        def close_tile(k, last, this, following):
            q, axial, swirl, ahead, behind = this
            if following is not None:
                ahead = [jnp.where(lane == LANES - 1, following[3][f], ahead[f]) for f in range(5)]
            if last is not None:
                first = last[4]
            else:
                first = [behind_ref[f, plane, rows] for f in range(5)]
                for f in range(5):
                    ahead_ref[f, plane, rows] = this[3][f]
            behind = [jnp.where(lane == 0, first[f], behind[f]) for f in range(5)]
            sponge = levels_ref[slot, rows, k * LANES : (k + 1) * LANES].astype(jnp.float32) * (
                time_step * sponge_rate
            )
            target = [
                jnp.broadcast_to(target_ref[f : f + 1, (k + 1) * LANES : (k + 2) * LANES], (chunk, LANES))
                for f in range(5)
            ]
            around = wide(2, k)
            scaled = [around * flux for flux in swirl]
            base = base_update(q, sponge, target, ahead, behind, wide(0, k), wide(1, k), scaled, cells)
            finish(plane, parity, start, k, axial)
            for f in range(5):
                base_ref[f, k, rows] = base[f]
                axial_refs[parity][f, k, rows] = axial[f]
                swirl_refs[parity][f, k, pl.ds(start + 8, chunk)] = scaled[f]

        opened = [open_tile(0)]
        for k in range(tiles):
            if k + 1 < tiles:
                opened.append(open_tile(k + 1))
            close_tile(
                k, opened[k - 1] if k else None, opened[k], opened[k + 1] if k + 1 < tiles else None
            )

    def one_plane(plane, parity):
        fetch(plane).wait()
        for f in range(5):
            for side, row in ((0, 7), (1, columns + 8)):
                edge = halo_ref[side, f, pl.ds(plane, 1), :]
                for k in range(tiles):
                    around = rows_ref[2, 0:1, k * LANES : (k + 1) * LANES]
                    swirl_refs[parity][f, k, row : row + 1] = around * edge[:, (k + 1) * LANES : (k + 2) * LANES]
        pl.when(plane > OUT_SLOTS)(lambda: store(plane - 1 - OUT_SLOTS).wait())

        def step(c, _):
            one_chunk(plane, parity, c)
            return 0

        lax.fori_loop(0, columns // chunk, step, 0, unroll=unroll)
        outer = jnp.logical_and(plane == 1, odd == 0)
        pl.when(outer)(lambda: keep(plane - 1).start())
        pl.when(jnp.logical_and(plane > 0, jnp.logical_not(outer)))(lambda: store(plane - 1).start())

        @pl.when(plane + IN_SLOTS < planes)
        def _():
            fetch(plane + IN_SLOTS).start()

    def two_planes(pair, _):
        for parity in range(2):
            one_plane(2 * pair + parity, parity)
        return 0

    lax.fori_loop(0, planes // 2, two_planes, 0)
    store(planes - 1 - OUT_SLOTS).wait()

    def last(c, _):
        start = pl.multiple_of(c * chunk, chunk)
        axial = outside(c, odd == 0)
        for k in range(tiles):
            finish(planes, 0, start, k, axial[k])
        return 0

    lax.fori_loop(0, columns // chunk, last, 0)
    pl.when(odd == 0)(lambda: store(planes - 1).start())
    pl.when(odd == 1)(lambda: keep(planes - 1).start())
    for plane in range(planes - OUT_SLOTS, planes):
        store(plane).wait()


def bulk_update(state, sponge, inv_dr, target, factor, near, halo, behind, cells, chunk=8, unroll=16):
    _, planes, columns, cycles = state.shape
    tiles = cycles // LANES - 1
    width = cycles - LANES
    return pl.pallas_call(
        functools.partial(update_kernel, cells=cells, chunk=chunk, unroll=unroll),
        in_specs=[VMEM_SPEC] * 7 + [HBM_SPEC],
        out_specs=[HBM_SPEC, VMEM_SPEC, VMEM_SPEC],
        scratch_shapes=[
            pltpu.VMEM((3, 8, width), jnp.float32),
            pltpu.VMEM((IN_SLOTS, columns, width), jnp.int32),
            pltpu.VMEM((OUT_SLOTS, 5, columns, width), jnp.float32),
            pltpu.VMEM((5, tiles, columns, LANES), jnp.float32),
            pltpu.VMEM((5, tiles, columns, LANES), jnp.float32),
            pltpu.VMEM((5, tiles, columns + 16, LANES), jnp.float32),
            pltpu.VMEM((5, tiles, columns + 16, LANES), jnp.float32),
            pltpu.VMEM((5, tiles, columns, LANES), jnp.float32),
            pltpu.SemaphoreType.DMA((IN_SLOTS,)),
            pltpu.SemaphoreType.DMA((OUT_SLOTS,)),
        ],
        out_shape=[
            jax.ShapeDtypeStruct(state.shape, jnp.float32),
            pltpu.VMEM((5, planes, columns, LANES), jnp.float32),
            pltpu.VMEM((5, columns, width), jnp.float32),
        ],
        compiler_params=pltpu.CompilerParams(vmem_limit_bytes=10 * MIB),
        input_output_aliases={5: 1},
        name="bulk_update",
    )(inv_dr, target, resident(factor), resident(near), resident(halo), resident(behind), resident(state), stored(sponge))


def filter_kernel(
    cutoff_ref, table_ref, inv_dr_ref, factor_ref, tile_ref, ahead_ref, halo_ref, flux_ref, rest_ref, *refs, cells,
):
    *sums, state_ref, out_ref, result_ref, outer_ref, split_ref, result_sem, outer_sem = refs
    _, planes, columns, cycles = out_ref.shape
    steps = planes // PACK
    half = table_ref.shape[2] // 4
    odd, sector = place()
    table = table_ref[sector]

    factor = factor_ref[odd * (planes - 1)][0:1]
    factor = jnp.where(odd == 1, -factor, factor)
    for f in range(5):
        for k in range(cycles // LANES - 1):
            cut = slice(k * LANES, (k + 1) * LANES)
            outer_ref[f, :, cut] = rest_ref[f, :, cut] + factor * flux_ref[f, :, cut]
    outer = pltpu.make_async_copy(
        outer_ref, out_ref.at[:, odd * (planes - 1), :, pl.ds(LANES, cycles - LANES)], outer_sem.at[0]
    )
    outer.start()

    weight = mode_weight(cutoff_ref[...], half, cells)
    lane = lax.broadcasted_iota(jnp.int32, (columns, LANES), 1)
    spacing = 4.0 / cycles
    edge = 1.0 + spacing * (LANES - 1)
    up = (0.5 * time_step) * inv_dr_ref[0:1, :LANES] * ((edge + spacing) / edge)
    up = jnp.where(lane == LANES - 1, up, 0.0)
    cycle = lax.broadcasted_iota(jnp.int32, (1, LANES), 1)
    around = (time_step * cells / (4.0 * math.pi)) / (1.0 + spacing * cycle.astype(jnp.float32))
    around = jnp.where(cycle < CYCLE, 0.0, around)

    def put(step, f):
        return pltpu.make_async_copy(
            result_ref.at[step % 2, f],
            out_ref.at[f, pl.ds(step * PACK, PACK), :, pl.ds(0, LANES)],
            result_sem.at[step % 2, f],
        )

    for step in range(steps):
        for f in range(5):
            group = step * 5 + f
            values = turn_back(
                sums, group * half, steps * 5 * half + group, weight, table, split_ref.at[group % 2], cells
            )
            if step >= 2:
                put(step - 2, f).wait()
            for i in range(PACK):
                turned = values if i == 0 else pltpu.roll(values, LANES - i * CYCLE, 1)
                plane = step * PACK + i
                value = tile_ref[f, plane] - up * ahead_ref[f, plane]
                value = jnp.where(lane < CYCLE, turned, value)
                low = value[0:1] + around * halo_ref[0, f, plane : plane + 1, :LANES]
                high = value[columns - 1 : columns] - around * halo_ref[1, f, plane : plane + 1, :LANES]
                result_ref[step % 2, f, i] = value
                result_ref[step % 2, f, i, 0:1] = low
                result_ref[step % 2, f, i, columns - 1 : columns] = high
            put(step, f).start()
    for step in range(max(steps - 2, 0), steps):
        for f in range(5):
            put(step, f).wait()
    outer.wait()


def put_filtered(cutoff, table, inv_dr, factor, tile, ahead, halo, flux, rest, sums, updated, cells):
    _, planes, columns, cycles = updated.shape
    return pl.pallas_call(
        functools.partial(filter_kernel, cells=cells),
        in_specs=[VMEM_SPEC] * (9 + len(sums)) + [HBM_SPEC],
        out_specs=HBM_SPEC,
        scratch_shapes=[
            pltpu.VMEM((2, 5, PACK, columns, LANES), jnp.float32),
            pltpu.VMEM((5, columns, cycles - LANES), jnp.float32),
            pltpu.VMEM((2, table.shape[2], LANES), jnp.bfloat16),
            pltpu.SemaphoreType.DMA((2, 5)),
            pltpu.SemaphoreType.DMA((1,)),
        ],
        out_shape=jax.ShapeDtypeStruct(updated.shape, jnp.float32),
        input_output_aliases={9 + len(sums): 0},
        compiler_params=pltpu.CompilerParams(vmem_limit_bytes=6 * MIB),
        name="put_filtered",
    )(
        cutoff, table, inv_dr, resident(factor), resident(tile), resident(ahead), resident(halo), resident(flux),
        resident(rest), *(resident(part) for part in sums), updated,
    )


def turn_back(sums, base, mean_row, weight, table, split_ref, cells):
    half = weight.shape[0]
    coefficient = sums[0][pl.ds(base, half), :]
    mean = sums[0][pl.ds(mean_row, 1), :]
    for other in sums[1:]:
        coefficient = coefficient + other[pl.ds(base, half), :]
        mean = mean + other[pl.ds(mean_row, 1), :]
    coefficient = coefficient * weight
    high = coefficient.astype(jnp.bfloat16)
    low = (coefficient - high.astype(jnp.float32)).astype(jnp.bfloat16)
    for k in range(2):
        split_ref[2 * k * half : (2 * k + 1) * half] = high
        split_ref[(2 * k + 1) * half : (2 * k + 2) * half] = low
    return jnp.dot(table, split_ref[...], preferred_element_type=jnp.float32) + mean * (1.0 / cells)


def mode_weight(cutoff, half, cells):
    count = half // 2
    mode = lax.broadcasted_iota(jnp.int32, (half, LANES), 0)
    mode = jnp.where(mode >= count, mode - count, mode) + 1
    return jnp.where(mode <= jnp.concatenate([cutoff] * PACK, axis=1), 2.0 / cells, 0.0)


def mode_tables(cells, sectors):
    columns = cells // sectors
    mode = np.arange(1, cells // 8 + 1)

    def waves(cell):
        angle = 2.0 * np.pi / cells * ((mode[:, None] * cell[None, :]) % cells)
        return np.concatenate([np.cos(angle), np.sin(angle)])

    forward, inverse, edge = [], [], []
    for sector in range(sectors):
        wave = waves(sector * columns + np.arange(columns))
        high = wave.astype(ml_dtypes.bfloat16)
        low = (wave - high.astype(np.float64)).astype(ml_dtypes.bfloat16)
        forward.append(np.block([[high, high], [low, low]]))
        inverse.append(np.concatenate([high.T, high.T, low.T, low.T], axis=1))
        ends = waves(np.array([sector * columns - 1, (sector + 1) * columns]) % cells)
        edge.append(np.broadcast_to(ends.T[:, :, None], (2, ends.shape[0], LANES)))
    return np.stack(forward), np.stack(inverse), np.stack(edge).astype(np.float32)


def body(forward, inverse, edge, cells, state, sponge_level, inv_dx, inv_dr, target, cutoff):
    sectors = lax.axis_size("az")
    rows = lax.axis_size("gx")
    cycles = state.shape[3]
    inv_dr = inv_dr.reshape(1, cycles)
    cutoff = cutoff.reshape(1, CYCLE)

    near_pairs = [(i ^ 1, i) for i in range(rows) if i ^ 1 < rows]
    far_pairs = [(i, i + 1) for i in range(1, rows - 1, 2)] + [(i + 1, i) for i in range(1, rows - 1, 2)]
    shifted = lambda part, by: lax.ppermute(part, "az", [(i, (i + by) % sectors) for i in range(sectors)])

    edges, far_first, far_rest, near_flux, factor = edge_cells(state, inv_dx)
    far_first = lax.ppermute(far_first, "gx", far_pairs)
    near_flux = lax.ppermute(near_flux, "gx", near_pairs)
    if sectors == 2:
        halo = shifted(edges, 1)
    else:
        halo = jnp.stack([shifted(edges[0], 1), shifted(edges[1], sectors - 1)])
    modes = functools.partial(
        inner_modes, sponge_level, inv_dr, target, factor, forward, edge, state, cells
    )
    middle = modes()
    far_rest = lax.ppermute(gate(far_rest, middle[0]), "gx", far_pairs)
    sums, tile, behind = modes(near=near_flux, far=far_first, after=halo, done=middle)
    others = [shifted(sums, by) for by in range(1, sectors)]
    updated, ahead, rest = bulk_update(
        state, sponge_level, inv_dr, target, factor, near_flux, halo, behind, cells
    )
    return put_filtered(
        cutoff, inverse, inv_dr, factor, tile, ahead, halo, far_rest, rest, [sums, *others],
        updated, cells,
    )


def solution(mesh):
    def whole(state, sponge_level, inv_dx, inv_dr, target, cutoff):
        cells = state.shape[2]
        tables = mode_tables(cells, mesh.shape["az"])
        mapped = jax.shard_map(
            functools.partial(body, *(jnp.asarray(table) for table in tables), cells),
            mesh=mesh,
            in_specs=(P(None, "gx", "az", None), P("gx", "az", None), P("gx"), P(), P(), P()),
            out_specs=P(None, "gx", "az", None),
            check_vma=False,
        )
        return mapped(state, sponge_level, inv_dx, inv_dr, target, cutoff)

    return whole
```
